32 devices in a mesh: batch: 4 (over x, core), ctx: 2 (over y), head: 4 (over z).
Axes of the slice: x: 2, y: 2, z: 4, core: 2. Of those that a mesh axis runs over, the one named last changes fastest.
Arguments:
- query_raw: bfloat16 [4096, 2560], P(('batch', 'ctx'), 'head'), parts along dimension 0, may hold values from -400 to 400
- key_raw: bfloat16 [4096, 2560], P(('batch', 'ctx'), 'head'), parts along dimension 0, may hold values from -400 to 400
- value_rows: bfloat16 [4096, 2560], P(('batch', 'ctx'), 'head'), parts along dimension 0, may hold values from -6 to 6
- query_gain: float32 [2560], P('head'), may hold values from 1.2 to 2
- key_gain: float32 [2560], P('head'), may hold values from 1.2 to 2
- segment: int32 [4096], P(('batch', 'ctx')), parts along dimension 0, may hold values from 0 to 5, never falling along the last dimension, each value on 1 to 512 neighbouring positions
- destination: int32 [4096], P(('batch', 'ctx')), parts along dimension 0, may hold values from 0 to 1023, as said below
- timestep: int32 [24], P('batch'), parts along dimension 0, may hold values from 0 to 49
- out_weight: bfloat16 [2560, 5120], P('head'), may hold values from -0.3125 to 0.3125
- gate_table: float32 [50, 5120], P(None, 'head'), may hold values from 0.5 to 1.5
Outputs:
- gated: bfloat16 [4096, 5120], P(('batch', 'ctx'), 'head'), parts along dimension 0
The draws below stay inside these ranges and needn't reach their ends.
There are 4 independent parts, one for each index of `batch`. The reference program is written for one: setup_inputs(seed, part) draws one part's arguments, and reference() takes and returns one part's arrays. A program takes and returns all parts, laid end to end along the dimension named above; an argument that names none is the same for every part. Nothing has to cross between parts.
Inputs may be any that keep to these rules, and one draw needn't show every extreme that they name: `segment`: the positions of one video are contiguous and the numbers never fall; each of the 6 videos has 1 to 512 positions, some video exactly 512. `destination`: A permutation of the 1024 rows. The 512 positions of each block b of 512 go 256 to every block c, and fill rows c*512 + b*256 to c*512 + (b+1)*256 - 1.
All inputs are finite; a program needn't handle non-finite values.
Results may differ from the reference program's by a relative error of at most 0.01555.
Values may be sent and summed in bfloat16 or wider, within the bound.
No kernel may reach another device: no remote copies, remote signals or barrier semaphores. Data moves between devices by JAX's collectives and lax.ppermute only.
A program may use at most 192 MiB of HBM per device.

```python
import math
import jax
import jax.numpy as jnp
import numpy as np
from jax import lax

D = 5120
HEADS = 20
HD = 128
STEPS = 50
VIDEOS = 6
TOK_DEV = 512
WIDTH = 2560
TOKENS = 1024
MAXLEN = 512
N_HEAD = 4


def column_scales(key):
    spread = jax.random.uniform(jax.random.fold_in(key, 11), (WIDTH,), jnp.float32, 0.0, math.log(10.0))
    placing = jnp.arange(WIDTH).astype(jnp.float32) / (WIDTH - 1)
    return jnp.exp(spread + placing * math.log(3.0)) / 3.0


def raw_field(key, which):
    inner_key = jax.random.fold_in(key, which)
    entries = jnp.clip(jax.random.normal(jax.random.fold_in(inner_key, 2), (TOKENS, WIDTH), jnp.float32), -4.0, 4.0)
    row_scale = jnp.exp(jax.random.uniform(jax.random.fold_in(inner_key, 1), (TOKENS, 1), jnp.float32, 0.0, math.log(10.0)))
    return entries * row_scale * column_scales(key)[None, :]


def draw_query_raw(key, part):
    result = raw_field(key, 1)
    return result.astype(jnp.bfloat16)


def draw_key_raw(key, part):
    result = raw_field(key, 2)
    return result.astype(jnp.bfloat16)


def draw_destination(key, part):
    blocks = TOKENS // TOK_DEV
    block_keys = jax.random.split(jax.random.fold_in(key, 5), blocks)
    orders = jax.vmap(lambda one_key: jax.random.permutation(one_key, TOK_DEV))(block_keys)
    slot_count = TOK_DEV // blocks
    sources = jnp.arange(blocks)[:, None]
    targets = orders % blocks
    within = orders // blocks
    result = targets * TOK_DEV + sources * slot_count + within
    return result.reshape(TOKENS).astype(jnp.int32)


def set_ends(values, rng, least, high):
    longest = values.shape.index(max(values.shape))
    spots = []
    for shift in (0, 1):
        where = [jax.random.randint(jax.random.fold_in(rng, axis), (), 0, length) for axis, length in enumerate(values.shape)]
        where[longest] = (where[longest] + shift) % values.shape[longest]
        spots.append(tuple(where))
    return values.at[spots[0]].set(least).at[spots[1]].set(high)


def with_spikes(values, own_key, source, target, parts, factor):
    def block_of(position):
        return (jnp.arange(values.shape[position]) // (values.shape[position] // parts)).reshape((-1,) + (1,) * (values.ndim - 1 - position))

    first = jax.random.permutation(own_key, parts)[block_of(target)]
    far = (block_of(target) + parts // 2) % parts
    return jnp.where((block_of(source) == first) | (block_of(source) == far), factor * values, values)


def steps_of(key, extent, pieces, low, top_value):
    gain = 1.0
    for position, parts in pieces:
        draws = jax.random.uniform(jax.random.fold_in(jax.random.fold_in(key, 6), position), (parts,), jnp.float32, low / len(pieces), top_value / len(pieces))
        gain = gain * jnp.repeat(jnp.exp(draws), extent[position] // parts).reshape((-1,) + (1,) * (len(extent) - 1 - position))
    return gain


def profile(amount, total, most, skew):
    weights = [(1 << 20) // math.isqrt(grade ** skew) + 1 for grade in range(2, amount + 1)]
    rest, given = total - most - (amount - 1), [1] * (amount - 1)
    while rest > 0:
        free = [i for i in range(amount - 1) if given[i] < most]
        pool, left = sum([weights[i] for i in free]), rest
        for i in free:
            more = min(most - given[i], max(1, left * weights[i] // pool), rest)
            given[i] = given[i] + more
            rest = rest - more
    return np.array([most] + given)


def uneven(stream_key, count, total, most, lean):
    if count == 2:
        one = jax.random.randint(stream_key, (), max(1, total - most), min(most, total - 1) + 1)
        return jnp.stack([one, total - one])
    sizes = jnp.asarray(profile(count, total, most, lean), jnp.int32)
    pairs = (count - 1) // 2
    donor, sink = sizes[1:1 + 2 * pairs:2], sizes[2:2 + 2 * pairs:2]
    slack = jnp.minimum(donor - 1, most - sink)
    moved = jax.random.randint(jax.random.fold_in(stream_key, 1), (pairs,), 0, 1 << 20) % (slack + 1)
    sizes = sizes.at[1:1 + 2 * pairs:2].set(donor - moved).at[2:2 + 2 * pairs:2].set(sink + moved)
    return sizes[jax.random.permutation(jax.random.fold_in(stream_key, 2), count)]


def bell_draw(rng, extent, scale, limit, shards=(), kind=jnp.bfloat16):
    values = jax.random.normal(rng, extent, jnp.float32) * scale
    if len(shards) > 0:
        values = steps_of(rng, extent, shards, -0.22, 0.18) * values
    return jnp.clip(values, min=-limit, max=limit).astype(kind)


def heavy_noise(key, shape, width, bound, cuts, heavy, kind=jnp.bfloat16):
    values = width * jax.random.normal(key, shape, jnp.float32)
    if cuts:
        values = values * steps_of(key, shape, cuts, -0.22, 0.18)
    return jnp.clip(with_spikes(values, jax.random.fold_in(key, 3), *heavy), -bound, bound).astype(kind)


def setup_inputs(seed: int = 0, part: int = 0) -> dict:
    key_of = jax.random.split(jax.random.key(seed), 11)
    own_keys = jax.random.split(jax.random.fold_in(key_of[10], part), 11)
    query_raw = draw_query_raw(jax.random.fold_in(jax.random.fold_in(key_of[10], part), 71), part)
    key_raw = draw_key_raw(jax.random.fold_in(jax.random.fold_in(key_of[10], part), 71), part)
    value_rows = bell_draw(own_keys[2], (TOKENS, WIDTH), 1.0, 6.0, ((0, 2), (1, 4)))
    query_gain = jnp.clip(1.2 + 0.79999995 * jax.random.uniform(key_of[3], (WIDTH,), jnp.float32) ** steps_of(key_of[3], (WIDTH,), ((0, 4),), -0.2, 0.2), 1.2, 2.0)
    key_gain = jnp.clip(1.2 + 0.79999995 * jax.random.uniform(key_of[4], (WIDTH,), jnp.float32) ** steps_of(key_of[4], (WIDTH,), ((0, 4),), -0.2, 0.2), 1.2, 2.0)
    segment = jnp.searchsorted(jnp.cumsum(uneven(own_keys[5], VIDEOS, TOKENS, MAXLEN, 2)), jnp.arange(TOKENS), side="right").astype(jnp.int32)
    destination = draw_destination(jax.random.fold_in(jax.random.fold_in(key_of[10], part), 71), part)
    timestep = set_ends(jax.random.randint(own_keys[7], (VIDEOS,), 0, STEPS), jax.random.fold_in(own_keys[7], 1), 0, STEPS - 1).astype(jnp.int32)
    out_weight = heavy_noise(key_of[8], (WIDTH, D), (WIDTH // 4) ** -0.5, 0.3125, ((0, 4),), (0, 1, 4, 2.0))
    gate_table = jnp.clip(0.5 + 1.0 * jax.random.uniform(key_of[9], (STEPS, D), jnp.float32) ** steps_of(key_of[9], (STEPS, D), ((1, 4),), -0.2, 0.2), 0.5, 1.5)
    return {"query_raw": query_raw, "key_raw": key_raw, "value_rows": value_rows, "query_gain": query_gain, "key_gain": key_gain, "segment": segment, "destination": destination, "timestep": timestep, "out_weight": out_weight, "gate_table": gate_table}


def normalize(raw_rows, gain_row):
    floats = raw_rows.astype(jnp.float32)
    mean_square = lax.optimization_barrier(jnp.mean(floats * floats, axis=1, keepdims=True))
    return (floats * lax.rsqrt(mean_square + 1e-06) * gain_row).astype(jnp.bfloat16)

def reference(query_raw, key_raw, value_rows, query_gain, key_gain, segment, destination, timestep, out_weight, gate_table):
    queries = normalize(query_raw, query_gain)
    normed_keys = normalize(key_raw, key_gain)
    score_scale = 1.0 / math.sqrt(HD)
    query_heads = queries.astype(jnp.float32).reshape(TOKENS, HEADS, HD)
    key_heads = normed_keys.astype(jnp.float32).reshape(TOKENS, HEADS, HD)
    value_heads = value_rows.astype(jnp.float32).reshape(TOKENS, HEADS, HD)
    block_rows = min(TOK_DEV, 256)

    def attend_block(first_row):
        block_queries = lax.dynamic_slice_in_dim(query_heads, first_row, block_rows, 0)
        block_marks = lax.dynamic_slice_in_dim(segment, first_row, block_rows, 0)
        scores = jnp.einsum('qhd,khd->hqk', block_queries, key_heads) * score_scale
        allowed = (block_marks[:, None] == segment[None, :])[None]
        scores = jnp.where(allowed, scores, -jnp.inf)
        largest = lax.optimization_barrier(jnp.max(scores, axis=2, keepdims=True))
        exponent = jnp.exp(scores - largest)
        totals = lax.optimization_barrier(jnp.sum(exponent, axis=2))
        weights = lax.optimization_barrier(exponent.astype(jnp.bfloat16)).astype(jnp.float32)
        output = jnp.einsum('hqk,khd->qhd', weights, value_heads) / jnp.transpose(totals)[:, :, None]
        return output.reshape(block_rows, HEADS * HD).astype(jnp.bfloat16)
    starts = (jnp.arange(TOKENS // block_rows) * block_rows).astype(jnp.int32)
    attended = lax.map(attend_block, starts).reshape(TOKENS, HEADS * HD)
    group_width = HEADS * HD // N_HEAD
    mixed_rows = jnp.zeros((TOKENS, D), jnp.float32)
    for member in range(N_HEAD):
        partial_value = jnp.dot(attended[:, member * group_width:(member + 1) * group_width], out_weight[member * group_width:(member + 1) * group_width], preferred_element_type=jnp.float32)
        mixed_rows = mixed_rows + lax.optimization_barrier(partial_value.astype(jnp.bfloat16)).astype(jnp.float32)
    owned = jnp.zeros_like(mixed_rows).at[destination].set(mixed_rows)
    owned_video = jnp.zeros_like(segment).at[destination].set(segment)
    video_gates = jnp.dot(jax.nn.one_hot(timestep, STEPS, dtype=jnp.float32), gate_table, precision=lax.Precision.HIGHEST)
    token_gates = jnp.dot(jax.nn.one_hot(owned_video, VIDEOS, dtype=jnp.float32), video_gates, precision=lax.Precision.HIGHEST)
    return (owned * token_gates).astype(jnp.bfloat16)
```

```python
import functools
import math

import jax
import jax.numpy as jnp
from jax import lax
from jax.experimental import pallas as pl
from jax.experimental.pallas import tpu as pltpu
from jax.sharding import PartitionSpec as P

HD = 128
F32 = jnp.float32
BF16 = jnp.bfloat16
VMEM = pl.BlockSpec(memory_space=pltpu.VMEM)
SMEM = pl.BlockSpec(memory_space=pltpu.SMEM)
ANY = pl.BlockSpec(memory_space=pl.ANY)
LIMIT = 48 * 1024 * 1024
HEAD_SPLIT = (2, 2, 1)

SWAP_CTX = ((0, 1), (1, 0))
SWAP_CORE = ((0, 1), (1, 0), (2, 3), (3, 2))
SWAP_X = ((0, 2), (2, 0), (1, 3), (3, 1))


def xor_pairs(size, step):
    return tuple((i, i ^ step) for i in range(size))


def params(**more):
    return pltpu.CompilerParams(vmem_limit_bytes=LIMIT, **more)


def cost(flops, moved):
    return pl.CostEstimate(flops=int(flops), bytes_accessed=int(moved), transcendentals=0)


def prepare_kernel(cuts, place, q_ref, k_ref, v_ref, dest_ref, seg_ref, own_ref, *outs):
    packed, stats_ref = outs[:-1], outs[-1]
    rows, width = q_ref.shape
    half = rows // 2
    me = place[0]
    dest = dest_ref[...]
    block = (dest >= rows).astype(jnp.int32)
    slot = dest - block * rows - me * half + jnp.where(block == me, 0, half)
    spread = (lax.broadcasted_iota(jnp.int32, (rows, rows), 0) == slot).astype(BF16)
    moved = jnp.dot(spread, q_ref[...], preferred_element_type=F32)
    moved_short = moved.astype(BF16)
    own_ref[...] = moved_short[:half]
    for ref, (low, high) in zip(packed, cuts):
        ref[0:half, :] = moved_short[half:, low:high]
        ref[half : half + rows, :] = k_ref[:, low:high]
        ref[half + rows :, :] = v_ref[:, low:high]
    keys = k_ref[...].astype(F32)
    ones = jnp.ones((8, width), F32)

    def row_sums(values):
        return lax.dot_general(
            ones, values * values, (((1,), (1,)), ((), ())),
            precision=lax.Precision.HIGHEST, preferred_element_type=F32,
        )

    marks = seg_ref[...].astype(F32)
    moved_marks = lax.dot_general(
        jnp.broadcast_to(marks, (8, rows)).astype(BF16), spread, (((1,), (1,)), ((), ())),
        preferred_element_type=F32,
    )
    stats_ref[0:1, :] = row_sums(moved)[0:1]
    stats_ref[1:2, :] = row_sums(keys)[0:1]
    stats_ref[2:3, :] = moved_marks[0:1]
    stats_ref[3:4, :] = marks
    stats_ref[4:8, :] = jnp.zeros((4, rows), F32)


def attend_kernel(
    heads, low, total_width, place, near_ref, far_ref, q_ref, remote_ref, k_ref, v_ref, qg_ref, kg_ref, out_ref
):
    rows = k_ref.shape[0]
    half = rows // 2
    me = place[0]
    stats = near_ref[...] + far_ref[...]
    q_sum = jnp.concatenate([stats[0:1, :half], stats[8:9, half:]], axis=1)
    q_mark = jnp.concatenate([stats[2:3, :half], stats[10:11, half:]], axis=1)
    k_sum = jnp.concatenate([stats[1:2], stats[9:10]], axis=1)
    k_mark = jnp.concatenate([stats[3:4], stats[11:12]], axis=1)

    def column(row):
        return jnp.transpose(jnp.broadcast_to(row, (8, row.shape[1])))[:, 0:1]

    q_factor = column(lax.rsqrt(q_sum / total_width + 1e-06))
    k_factor = column(lax.rsqrt(k_sum / total_width + 1e-06))
    allowed = column(q_mark) == k_mark
    scale = math.log2(math.e) / math.sqrt(HD)
    for head in range(heads):
        cut = slice(head * HD, (head + 1) * HD)
        wide = slice(low + head * HD, low + (head + 1) * HD)
        queries = jnp.concatenate([q_ref[:, wide], remote_ref[0:half, cut]], axis=0)
        keys = jnp.concatenate([k_ref[:, wide], remote_ref[half : half + rows, cut]], axis=0)
        values = jnp.concatenate([v_ref[:, wide], remote_ref[half + rows :, cut]], axis=0)
        queries = (queries.astype(F32) * q_factor * qg_ref[0:1, wide]).astype(BF16)
        keys = (keys.astype(F32) * k_factor * kg_ref[0:1, wide]).astype(BF16)
        for part in range(2):
            piece = slice(part * half, (part + 1) * half)
            scores = lax.dot_general(
                queries[piece], keys, (((1,), (1,)), ((), ())), preferred_element_type=F32
            )
            scores = jnp.where(allowed[piece], scores, -1e30)
            largest = jnp.max(scores, axis=1, keepdims=True)
            weights = jnp.exp2((scores - largest) * scale)
            totals = jnp.sum(weights, axis=1, keepdims=True)
            mixed = jnp.dot(weights.astype(BF16), values, preferred_element_type=F32)
            start = me * half if part == 0 else (1 - me) * half
            out_ref[pl.ds(pl.multiple_of(start, half), half), cut] = (mixed / totals).astype(BF16)


def cut_kernel(place, weight_ref, *refs):
    outs, sems = refs[:3], refs[3]
    rows, width = outs[0].shape
    first = pl.multiple_of(place[2] * rows, rows)
    copies = []
    for step in range(1, 4):
        column = pl.multiple_of((place[1] ^ step) * width, width)
        copies.append(
            pltpu.make_async_copy(
                weight_ref.at[pl.ds(first, rows), pl.ds(column, width)], outs[step - 1], sems.at[step - 1]
            )
        )
    for copy in copies:
        copy.start()
    for copy in copies:
        copy.wait()


def project_kernel(cuts, place, near_ref, far_ref, times, gate_ref, weight_ref, *refs):
    chunk_count = len(cuts)
    parts = refs[: 5 * chunk_count]
    shares = refs[5 * chunk_count : 5 * chunk_count + 8]
    out_ref, own_w, w_all, sems, total = refs[5 * chunk_count + 8 :]
    rows, width = out_ref.shape
    half = rows // 2
    group = own_w.shape[0]
    share = group // 8
    me, head, mine = place[0], place[1], place[2]
    own_copy = pltpu.make_async_copy(
        weight_ref.at[:, pl.ds(pl.multiple_of(head * width, width), width)], own_w, sems.at[0]
    )
    own_copy.start()
    copies = []
    for index in range(8):
        start = pl.multiple_of((mine ^ index) * share, share)
        for step in range(3):
            copies.append(
                pltpu.make_async_copy(
                    shares[index].at[pl.ds(step * share, share), :],
                    w_all.at[step, pl.ds(start, share), :],
                    sems.at[1 + index * 3 + step],
                )
            )
    for copy in copies:
        copy.start()
    own_copy.wait()
    total[...] = jnp.dot(parts[0][...], own_w[cuts[0][0] : cuts[0][1]], preferred_element_type=F32)
    for chunk, (low, high) in enumerate(cuts):
        if chunk > 0:
            total[...] += jnp.dot(parts[5 * chunk][...], own_w[low:high], preferred_element_type=F32)
    for copy in copies:
        copy.wait()
    inner = jnp.logical_or(head == 1, head == 2)
    for chunk, (low, high) in enumerate(cuts):
        own, one, two, three_near, three_far = parts[5 * chunk : 5 * chunk + 5]
        total[...] += jnp.dot(one[...], w_all[0, low:high], preferred_element_type=F32)
        total[...] += jnp.dot(two[...], w_all[1, low:high], preferred_element_type=F32)
        three = jnp.where(inner, three_near[...], three_far[...])
        total[...] += jnp.dot(three, w_all[2, low:high], preferred_element_type=F32)
    stats = near_ref[...] + far_ref[...]
    own_mark = stats[2:3, :half]
    other_mark = stats[10:11, half:]
    for part in range(2):
        row = own_mark if part == 0 else other_mark
        marks = jnp.transpose(jnp.broadcast_to(row, (8, half)))[:, 0:1]
        start = me * half if part == 0 else (1 - me) * half
        at = pl.ds(pl.multiple_of(start, half), half)
        gates = jnp.zeros((half, width), F32)
        for video in range(times.shape[0]):
            gate = gate_ref[pl.ds(times[video], 1), :]
            gates = jnp.where(marks == 4.0 * video, gate, gates)
        out_ref[at, :] = (total[at, :] * gates).astype(BF16)


def fast_local(
    query_raw, key_raw, value_rows, query_gain, key_gain, segment, destination, timestep, out_weight, gate_table
):
    rows, width = query_raw.shape
    half = rows // 2
    out_width = gate_table.shape[1]
    total_width = width * lax.axis_size("head")
    ctx, head, batch = lax.axis_index("ctx"), lax.axis_index("head"), lax.axis_index("batch")
    mine = batch * 2 + ctx
    place = jnp.stack([ctx, head, mine]).astype(jnp.int32)
    cuts, low = [], 0
    for count in HEAD_SPLIT:
        cuts.append((low * HD, (low + count) * HD))
        low += count
    assert low * HD == width
    share = width // 8

    cut_weights = pl.pallas_call(
        cut_kernel,
        in_specs=[SMEM, ANY],
        out_specs=[VMEM] * 3,
        out_shape=[jax.ShapeDtypeStruct((share, out_width), BF16)] * 3,
        scratch_shapes=[pltpu.SemaphoreType.DMA((3,))],
        compiler_params=params(),
        cost_estimate=cost(0, 6 * share * out_width * 2),
        name="cut_weights",
    )(place, out_weight)
    from_head = [lax.ppermute(cut_weights[s - 1], "head", xor_pairs(4, s)) for s in (1, 2, 3)]
    share0 = jnp.concatenate(from_head, axis=0)
    share_y = lax.ppermute(share0, "ctx", SWAP_CTX)
    share_x = lax.ppermute(share0, "batch", SWAP_X)
    share_xy = lax.ppermute(share_y, "batch", SWAP_X)
    shares = [None] * 8
    for index, value in ((0, share0), (1, share_y), (4, share_x), (5, share_xy)):
        shares[index] = value
        shares[index ^ 2] = lax.ppermute(value, "batch", SWAP_CORE)

    packed_shapes = [jax.ShapeDtypeStruct((half + 2 * rows, high - low), BF16) for low, high in cuts]
    own_queries, *packed, stats = pl.pallas_call(
        functools.partial(prepare_kernel, cuts),
        in_specs=[SMEM] + [VMEM] * 5,
        out_specs=[VMEM] * (2 + len(cuts)),
        out_shape=[jax.ShapeDtypeStruct((half, width), BF16)]
        + packed_shapes
        + [jax.ShapeDtypeStruct((8, rows), F32)],
        compiler_params=params(),
        cost_estimate=cost(2 * rows * rows * width, 6 * rows * width * 2),
        name="prepare",
    )(place, query_raw, key_raw, value_rows, destination.reshape(1, rows), segment.reshape(1, rows))

    other_stats = lax.ppermute(stats, "ctx", SWAP_CTX)
    both = jnp.concatenate([stats, other_stats], axis=0)
    near = both + lax.ppermute(both, "head", xor_pairs(4, 1))
    far = lax.ppermute(near, "head", xor_pairs(4, 2))

    arrived = [lax.ppermute(piece, "ctx", SWAP_CTX) for piece in packed]
    parts = []
    for (low, high), piece in zip(cuts, arrived):
        heads = (high - low) // HD
        attended = pl.pallas_call(
            functools.partial(attend_kernel, heads, low, total_width),
            in_specs=[SMEM] + [VMEM] * 8,
            out_specs=VMEM,
            out_shape=jax.ShapeDtypeStruct((rows, high - low), BF16),
            compiler_params=params(),
            cost_estimate=cost(heads * 3 * 4 * rows * 2 * rows * HD, 4 * rows * width * 2),
            name="attend",
        )(
            place, near, far, own_queries, piece, key_raw, value_rows,
            query_gain.reshape(1, width), key_gain.reshape(1, width),
        )
        one = lax.ppermute(attended, "head", xor_pairs(4, 1))
        three_near = lax.ppermute(attended, "head", ((1, 2), (2, 1)))
        two = lax.ppermute(attended, "head", xor_pairs(4, 2))
        three_far = lax.ppermute(two, "head", ((2, 3), (1, 0)))
        parts += [attended, one, two, three_near, three_far]

    return pl.pallas_call(
        functools.partial(project_kernel, cuts),
        in_specs=[SMEM, VMEM, VMEM, SMEM, VMEM, ANY] + [VMEM] * len(parts) + [ANY] * 8,
        out_specs=VMEM,
        out_shape=jax.ShapeDtypeStruct((rows, out_width), BF16),
        scratch_shapes=[
            pltpu.VMEM((width, out_width), BF16),
            pltpu.VMEM((3, width, out_width), BF16),
            pltpu.SemaphoreType.DMA((25,)),
            pltpu.VMEM((rows, out_width), F32),
        ],
        compiler_params=params(),
        cost_estimate=cost(2 * rows * 4 * width * out_width, 5 * width * out_width * 2),
        name="project",
    )(place, near, far, timestep, gate_table, out_weight, *parts, *shares)


def for_sending(array):

    def short(part):
        return part.astype(jnp.bfloat16) if part.dtype == jnp.float32 else part

    return jax.tree.map(short, array)


def attend(running, queries, query_mark, key_rows, value_part, key_mark, head_count, score_scale):
    maxima, totals, accumulated = running
    query_count = queries.shape[0]
    query_heads = queries.reshape(query_count, head_count, HD)
    key_heads = key_rows.reshape(key_rows.shape[0], head_count, HD)
    value_heads = value_part.reshape(value_part.shape[0], head_count, HD)
    scores = (
        jnp.einsum("qhd,khd->hqk", query_heads, key_heads, preferred_element_type=jnp.float32)
        * score_scale
    )
    allowed = (query_mark[:, None] == key_mark[None, :])[None]
    scores = jnp.where(allowed, scores, -1e30)
    new_max = jnp.maximum(maxima, jnp.max(scores, axis=2))
    factor = jnp.exp(maxima - new_max)
    weights = jnp.where(allowed, jnp.exp(scores - new_max[:, :, None]), 0.0)
    totals = totals * factor + jnp.sum(weights, axis=2)
    update = jnp.einsum(
        "hqk,khd->qhd",
        weights.astype(jnp.bfloat16),
        value_heads,
        preferred_element_type=jnp.float32,
    )
    accumulated = accumulated * jnp.transpose(factor)[:, :, None] + update
    return (new_max, totals, accumulated)


def attend_blocks(
    running, queries, query_mark, key_rows, value_part, key_mark, head_count, score_scale
):
    block_rows = queries.shape[0]
    block_count = key_rows.shape[0] // block_rows
    stacked = (
        key_rows.reshape(block_count, block_rows, key_rows.shape[1]),
        value_part.reshape(block_count, block_rows, value_part.shape[1]),
        key_mark.reshape(block_count, block_rows),
    )

    def advance(state, shard_piece):
        return (
            attend(
                state,
                queries,
                query_mark,
                shard_piece[0],
                shard_piece[1],
                shard_piece[2],
                head_count,
                score_scale,
            ),
            None,
        )

    running, unused = lax.scan(advance, running, stacked)
    return running


def general_local(
    query_raw,
    key_raw,
    value_rows,
    query_gain,
    key_gain,
    segment,
    destination,
    timestep,
    out_weight,
    gate_table,
):
    row_count = query_raw.shape[0]
    row_width = query_raw.shape[1]
    head_count = row_width // HD
    ctx_size = lax.axis_size("ctx")
    total_width = row_width * lax.axis_size("head")
    score_scale = 1.0 / math.sqrt(HD)
    query_float = query_raw.astype(jnp.float32)
    key_float = key_raw.astype(jnp.float32)
    query_sum, key_sum = lax.psum(
        (jnp.sum(query_float * query_float, axis=1), jnp.sum(key_float * key_float, axis=1)), "head"
    )
    queries = (
        query_float * lax.rsqrt(query_sum / total_width + 1e-06)[:, None] * query_gain
    ).astype(jnp.bfloat16)
    normed_keys = (key_float * lax.rsqrt(key_sum / total_width + 1e-06)[:, None] * key_gain).astype(
        jnp.bfloat16
    )
    slot_count = row_count // ctx_size
    target = destination // row_count * slot_count + destination % slot_count

    def placed(array):
        return jnp.zeros_like(array).at[target].set(array)

    initial = (
        jnp.full((head_count, row_count), -1e30, jnp.float32),
        jnp.zeros((head_count, row_count), jnp.float32),
        jnp.zeros((row_count, head_count, HD), jnp.float32),
    )
    own_queries, own_keys, own_values, own_segment = (
        lax.all_to_all(placed(queries), "ctx", split_axis=0, concat_axis=0, tiled=True),
        lax.all_to_all(placed(normed_keys), "ctx", split_axis=0, concat_axis=0, tiled=True),
        lax.all_to_all(placed(value_rows), "ctx", split_axis=0, concat_axis=0, tiled=True),
        lax.all_to_all(placed(segment), "ctx", split_axis=0, concat_axis=0, tiled=True),
    )
    running = attend_blocks(
        initial,
        own_queries,
        own_segment,
        lax.all_gather(own_keys, "ctx", axis=0, tiled=True),
        lax.all_gather(own_values, "ctx", axis=0, tiled=True),
        lax.all_gather(for_sending(own_segment), "ctx", axis=0, tiled=True),
        head_count,
        score_scale,
    )
    attended = (
        (running[2] / jnp.transpose(running[1])[:, :, None])
        .reshape(row_count, row_width)
        .astype(jnp.bfloat16)
    )
    head_terms = jnp.dot(attended, out_weight, preferred_element_type=jnp.float32)
    mixed_rows = lax.psum_scatter(
        head_terms.astype(jnp.bfloat16), "head", scatter_dimension=1, tiled=True
    ).astype(jnp.float32)
    video_gates = jnp.dot(
        jax.nn.one_hot(timestep, gate_table.shape[0], dtype=jnp.float32),
        gate_table,
        precision=lax.Precision.HIGHEST,
    )
    token_gates = jnp.dot(
        jax.nn.one_hot(own_segment, timestep.shape[0], dtype=jnp.float32),
        video_gates,
        precision=lax.Precision.HIGHEST,
    )
    return (mixed_rows * token_gates).astype(jnp.bfloat16)


def solution(mesh):
    placed = (
        P(("batch", "ctx"), "head"),
        P(("batch", "ctx"), "head"),
        P(("batch", "ctx"), "head"),
        P("head"),
        P("head"),
        P(("batch", "ctx")),
        P(("batch", "ctx")),
        P("batch"),
        P("head", None),
        P(None, "head"),
    )
    sizes = dict(mesh.shape)
    fast = sizes["batch"] == 4 and sizes["ctx"] == 2 and sizes["head"] == 4
    local = fast_local if fast else general_local
    return jax.shard_map(
        local, mesh=mesh, in_specs=placed, out_specs=P(("batch", "ctx"), "head"), check_vma=False
    )
```

```python
import functools
import math

import jax
import jax.numpy as jnp
from jax import lax
from jax.experimental import pallas as pl
from jax.experimental.pallas import tpu as pltpu
from jax.sharding import PartitionSpec as P

HD = 128
F32 = jnp.float32
BF16 = jnp.bfloat16
VMEM = pl.BlockSpec(memory_space=pltpu.VMEM)
SMEM = pl.BlockSpec(memory_space=pltpu.SMEM)
ANY = pl.BlockSpec(memory_space=pl.ANY)
HBM = pl.BlockSpec(memory_space=pltpu.HBM)
AFTER = VMEM
SENDS = (3, 2)

SWAP_CTX = ((0, 1), (1, 0))
SWAP_CORE = ((0, 1), (1, 0), (2, 3), (3, 2))
SWAP_X = ((0, 2), (2, 0), (1, 3), (3, 1))


def xor_pairs(size, step):
    return tuple((i, i ^ step) for i in range(size))


def params(mebibytes):
    return pltpu.CompilerParams(vmem_limit_bytes=mebibytes * 1024 * 1024)


def cost(microseconds):
    return pl.CostEstimate(flops=0, bytes_accessed=int(microseconds * 3_600_000), transcendentals=0)


def load(pairs, sems):
    copies = [pltpu.make_async_copy(source, target, sems.at[i]) for i, (source, target) in enumerate(pairs)]
    for copy in copies:
        copy.start()
    return copies


def row_sums(values):
    squares = values * values
    folded = squares[:, 0:HD]
    for low in range(HD, values.shape[1], HD):
        folded = folded + squares[:, low : low + HD]
    return jnp.sum(jnp.transpose(folded), axis=0, keepdims=True)


def three_pieces(value):
    pieces = []
    for _ in range(3):
        short = value.astype(BF16).astype(F32)
        pieces.append(short)
        value = value - short
    return pieces


def column(row):
    return jnp.transpose(jnp.broadcast_to(row, (8, row.shape[1])))[:, 0:1]


def prepare_kernel(
    cut, place, q_hbm, k_hbm, v_hbm, dest_hbm, seg_hbm, own_ref, other_ref, packed_ref, stats_ref, k_ref, v_ref,
    q_ref, dest_ref, seg_ref, sems,
):
    copies = load(
        ((dest_hbm, dest_ref), (seg_hbm, seg_ref), (q_hbm, q_ref), (k_hbm, k_ref), (v_hbm, v_ref)), sems
    )
    rows = q_ref.shape[0]
    half = rows // 2
    low, high = cut
    me = place[0]
    copies[0].wait()
    copies[1].wait()
    dest = dest_ref[...]
    block = (dest >= rows).astype(jnp.int32)
    slot = dest - block * rows - me * half + jnp.where(block == me, 0, half)
    spread = (lax.broadcasted_iota(jnp.int32, (rows, rows), 0) == slot).astype(BF16)
    marks = seg_ref[...].astype(F32)
    moved_marks = lax.dot_general(
        jnp.broadcast_to(marks, (8, rows)).astype(BF16), spread, (((1,), (1,)), ((), ())),
        preferred_element_type=F32,
    )[0:1]
    copies[2].wait()
    moved = jnp.dot(spread, q_ref[...], preferred_element_type=F32)
    moved_short = moved.astype(BF16)
    own_ref[...] = moved_short[:half]
    other_ref[...] = moved_short[half:]
    packed_ref[0:half, :] = moved_short[half:, low:high]
    query_sums = row_sums(moved)
    copies[3].wait()
    packed_ref[half : half + rows, :] = k_ref[:, low:high]
    key_sums = row_sums(k_ref[...].astype(F32))
    stats_ref[...] = jnp.concatenate(
        [query_sums, key_sums, moved_marks, marks, jnp.zeros((4, rows), F32)], axis=0
    )
    copies[4].wait()
    packed_ref[half + rows :, :] = v_ref[:, low:high]


def settle_kernel(near_ref, far_ref, *refs):
    refs[-1][...] = near_ref[...] + far_ref[...]


def pack_kernel(cut, other_ref, k_ref, v_ref, after_ref, out_ref):
    low, high = cut
    half, rows = other_ref.shape[0], k_ref.shape[0]
    out_ref[0:half, :] = other_ref[:, low:high]
    out_ref[half : half + rows, :] = k_ref[:, low:high]
    out_ref[half + rows :, :] = v_ref[:, low:high]


def attend_kernel(
    cut, total_width, place, near_ref, far_ref, q_ref, k_ref, v_ref, qg_ref, kg_ref, remote_ref, after_ref, out_ref
):
    rows = k_ref.shape[0]
    half = rows // 2
    me = place[0]
    near, far = near_ref[...], far_ref[...]
    near_factors = lax.rsqrt(near[0:2] / total_width + 1e-06)
    far_factors = lax.rsqrt(far[0:2] / total_width + 1e-06)
    q_mark = jnp.concatenate([near[2:3, :half], far[2:3, half:]], axis=1)
    k_mark = jnp.concatenate([near[3:4], far[3:4]], axis=1)
    q_factor = column(jnp.concatenate([near_factors[0:1, :half], far_factors[0:1, half:]], axis=1))
    k_factor = column(jnp.concatenate([near_factors[1:2], far_factors[1:2]], axis=1))
    allowed = column(q_mark) == k_mark
    scale = math.log2(math.e) / math.sqrt(HD)
    first, last = cut
    for low in range(first, last, HD):
        here = slice(low - first, low - first + HD)
        wide = slice(low, low + HD)
        queries = jnp.concatenate([q_ref[:, wide], remote_ref[0:half, here]], axis=0)
        keys = jnp.concatenate([k_ref[:, wide], remote_ref[half : half + rows, here]], axis=0)
        values = jnp.concatenate([v_ref[:, wide], remote_ref[half + rows :, here]], axis=0)
        queries = (queries.astype(F32) * q_factor * qg_ref[0:1, wide]).astype(BF16)
        keys = (keys.astype(F32) * k_factor * kg_ref[0:1, wide]).astype(BF16)
        for part in range(2):
            piece = slice(part * half, (part + 1) * half)
            scores = lax.dot_general(
                queries[piece], keys, (((1,), (1,)), ((), ())), preferred_element_type=F32
            )
            scores = jnp.where(allowed[piece], scores, -1e30)
            largest = jnp.max(scores, axis=1, keepdims=True)
            weights = jnp.exp2((scores - largest) * scale)
            totals = jnp.sum(weights, axis=1, keepdims=True)
            mixed = jnp.dot(weights.astype(BF16), values, preferred_element_type=F32)
            start = me * half if part == 0 else (1 - me) * half
            at = pl.ds(pl.multiple_of(start, half), half)
            out_ref[at, here] = (mixed / totals).astype(BF16)


def cut_kernel(place, weight_ref, *refs):
    outs, sems = refs[:3], refs[3]
    rows, width = outs[0].shape
    first = pl.multiple_of(place[2] * rows, rows)
    pairs = []
    for step in range(1, 4):
        start = pl.multiple_of((place[1] ^ step) * width, width)
        pairs.append((weight_ref.at[pl.ds(first, rows), pl.ds(start, width)], outs[step - 1]))
    for copy in load(pairs, sems):
        copy.wait()


def join_kernel(one_ref, two_ref, three_ref, after_ref, out_ref):
    share = one_ref.shape[0]
    for step, ref in enumerate((one_ref, two_ref, three_ref)):
        out_ref[step * share : (step + 1) * share, :] = ref[...]


def project_kernel(chunks, place, times, near_ref, far_ref, gate_ref, weight_ref, *refs):
    parts, shares = refs[: 4 * chunks], refs[4 * chunks : 4 * chunks + 8]
    out_hbm, rows_all, w_all, gates_ref, total, out_ref, sems = refs[4 * chunks + 8 :]
    rows, width = out_ref.shape
    half = rows // 2
    group = w_all.shape[0] // 4
    share = group // 8
    me, head, mine = place[0], place[1], place[2]
    own_start = pl.multiple_of(head * width, width)
    own_copy = pltpu.make_async_copy(
        weight_ref.at[:, pl.ds(own_start, width)], w_all.at[pl.ds(0, group), :], sems.at[0]
    )
    own_copy.start()
    low = 0
    for slot in range(4):
        for chunk in range(chunks):
            part = parts[4 * chunk + slot]
            rows_all[:, low : low + part.shape[1]] = part[...]
            low += part.shape[1]
    for step in range(3):
        for index in range(8):
            start = pl.multiple_of((1 + step) * group + (mine ^ index) * share, share)
            w_all[pl.ds(start, share), :] = shares[index][step * share : (step + 1) * share, :]
    gates_ref[...] = jnp.zeros(gates_ref.shape, BF16)
    for video in range(times.shape[0]):
        for index, piece in enumerate(three_pieces(gate_ref[pl.ds(times[video], 1), :])):
            gates_ref[index * 16 + video : index * 16 + video + 1, :] = piece.astype(BF16)
    videos = lax.rem(lax.broadcasted_iota(jnp.int32, (rows, gates_ref.shape[0]), 1), 16).astype(F32)
    own_mark, other_mark = near_ref[2:3, :half], far_ref[2:3, half:]
    marks = jnp.concatenate(
        [jnp.where(me == 0, own_mark, other_mark), jnp.where(me == 0, other_mark, own_mark)], axis=1
    )
    picked = (column(marks) == 4.0 * videos).astype(BF16)
    own_copy.wait()
    middle = 2 * group
    blocks = [slice(low, low + 256) for low in range(0, width, 256)]
    for block in blocks:
        total[:, block] = jnp.dot(rows_all[:, 0:middle], w_all[0:middle, block], preferred_element_type=F32)
    out_copies = []
    for index, block in enumerate(blocks):
        gates = jnp.dot(picked, gates_ref[:, block], preferred_element_type=F32)
        mixed = total[:, block] + jnp.dot(
            rows_all[:, middle:], w_all[middle:, block], preferred_element_type=F32
        )
        out_ref[:, block] = (mixed * gates).astype(BF16)
        out_copies.append(
            pltpu.make_async_copy(out_ref.at[:, block], out_hbm.at[:, block], sems.at[1 + index])
        )
        out_copies[-1].start()
    for copy in out_copies:
        copy.wait()


def fast_local(
    query_raw, key_raw, value_rows, query_gain, key_gain, segment, destination, timestep, out_weight, gate_table
):
    rows, width = query_raw.shape
    half = rows // 2
    out_width = gate_table.shape[1]
    total_width = width * lax.axis_size("head")
    ctx, head, batch = lax.axis_index("ctx"), lax.axis_index("head"), lax.axis_index("batch")
    mine = batch * 2 + ctx
    place = jnp.stack([ctx, head, mine]).astype(jnp.int32)
    cuts, low = [], 0
    for count in SENDS:
        cuts.append((low * HD, (low + count) * HD))
        low += count
    assert low * HD == width
    share = width // 8
    packed_shapes = [jax.ShapeDtypeStruct((half + 2 * rows, high - low), BF16) for low, high in cuts]
    in_hbm = functools.partial(pltpu.with_memory_space_constraint, memory_space=pltpu.HBM)
    weight_hbm = in_hbm(out_weight)

    cut_weights = pl.pallas_call(
        cut_kernel,
        in_specs=[SMEM, HBM],
        out_specs=[VMEM] * 3,
        out_shape=[jax.ShapeDtypeStruct((share, out_width), BF16)] * 3,
        scratch_shapes=[pltpu.SemaphoreType.DMA((3,))],
        compiler_params=params(4),
        cost_estimate=cost(1),
        name="cut_weights",
    )(place, weight_hbm)
    from_head = [lax.ppermute(cut_weights[s - 1], "head", xor_pairs(4, s)) for s in (1, 2, 3)]

    own_queries, other_queries, packed, stats, keys, values = pl.pallas_call(
        functools.partial(prepare_kernel, cuts[0]),
        in_specs=[SMEM] + [HBM] * 5,
        out_specs=[VMEM] * 6,
        out_shape=[
            jax.ShapeDtypeStruct((half, width), BF16),
            jax.ShapeDtypeStruct((half, width), BF16),
            packed_shapes[0],
            jax.ShapeDtypeStruct((8, rows), F32),
            jax.ShapeDtypeStruct((rows, width), BF16),
            jax.ShapeDtypeStruct((rows, width), BF16),
        ],
        scratch_shapes=[
            pltpu.VMEM((rows, width), BF16),
            pltpu.VMEM((1, rows), jnp.int32),
            pltpu.VMEM((1, rows), jnp.int32),
            pltpu.SemaphoreType.DMA((5,)),
        ],
        compiler_params=params(14),
        cost_estimate=cost(2),
        name="prepare",
    )(
        place, in_hbm(query_raw), in_hbm(key_raw), in_hbm(value_rows),
        in_hbm(destination.reshape(1, rows)), in_hbm(segment.reshape(1, rows)),
    )
    arrived = [lax.ppermute(packed, "ctx", SWAP_CTX)]
    stats = stats + lax.ppermute(stats, "head", xor_pairs(4, 1))
    near = pl.pallas_call(
        settle_kernel,
        in_specs=[VMEM] * 2 + [AFTER] * 4,
        out_specs=VMEM,
        out_shape=jax.ShapeDtypeStruct((8, rows), F32),
        compiler_params=params(4),
        cost_estimate=cost(1),
        name="settle",
    )(stats, lax.ppermute(stats, "head", xor_pairs(4, 2)), arrived[0], *from_head)
    far = lax.ppermute(near, "ctx", SWAP_CTX)
    packed = pl.pallas_call(
        functools.partial(pack_kernel, cuts[1]),
        in_specs=[VMEM] * 3 + [AFTER],
        out_specs=VMEM,
        out_shape=packed_shapes[1],
        compiler_params=params(4),
        cost_estimate=cost(1),
        name="pack",
    )(other_queries, keys, values, far)
    arrived.append(lax.ppermute(packed, "ctx", SWAP_CTX))

    parts = []
    before = near
    for cut, piece in zip(cuts, arrived):
        attended = pl.pallas_call(
            functools.partial(attend_kernel, cut, total_width),
            in_specs=[SMEM] + [VMEM] * 8 + [AFTER],
            out_specs=VMEM,
            out_shape=jax.ShapeDtypeStruct((rows, cut[1] - cut[0]), BF16),
            compiler_params=params(14),
            cost_estimate=cost(8),
            name="attend",
        )(
            place, near, far, own_queries, keys, values, query_gain.reshape(1, width),
            key_gain.reshape(1, width), piece, before,
        )
        one = lax.ppermute(attended, "head", xor_pairs(4, 1))
        two = lax.ppermute(attended, "head", xor_pairs(4, 2))
        three = lax.ppermute(two, "head", xor_pairs(4, 1))
        parts += [attended, one, two, three]
        before = attended

    share0 = pl.pallas_call(
        join_kernel,
        in_specs=[VMEM] * 3 + [AFTER],
        out_specs=VMEM,
        out_shape=jax.ShapeDtypeStruct((3 * share, out_width), BF16),
        compiler_params=params(4),
        cost_estimate=cost(1),
        name="join",
    )(*from_head, parts[0])
    share_y = lax.ppermute(share0, "ctx", SWAP_CTX)
    share_x = lax.ppermute(share0, "batch", SWAP_X)
    share_xy = lax.ppermute(share_y, "batch", SWAP_X)
    shares = [None] * 8
    for index, value in ((0, share0), (1, share_y), (4, share_x), (5, share_xy)):
        shares[index] = value
        shares[index ^ 2] = lax.ppermute(value, "batch", SWAP_CORE)

    return pl.pallas_call(
        functools.partial(project_kernel, 2),
        in_specs=[SMEM, SMEM] + [VMEM] * 3 + [HBM] + [VMEM] * (len(parts) + 8),
        out_specs=ANY,
        out_shape=jax.ShapeDtypeStruct((rows, out_width), BF16),
        scratch_shapes=[
            pltpu.VMEM((rows, 4 * width), BF16),
            pltpu.VMEM((4 * width, out_width), BF16),
            pltpu.VMEM((48, out_width), BF16),
            pltpu.VMEM((rows, out_width), F32),
            pltpu.VMEM((rows, out_width), BF16),
            pltpu.SemaphoreType.DMA((1 + out_width // 256,)),
        ],
        compiler_params=params(28),
        cost_estimate=cost(8),
        name="project",
    )(place, timestep, near, far, gate_table, weight_hbm, *parts, *shares)


def for_sending(array):

    def short(part):
        return part.astype(jnp.bfloat16) if part.dtype == jnp.float32 else part

    return jax.tree.map(short, array)


def attend(running, queries, query_mark, key_rows, value_part, key_mark, head_count, score_scale):
    maxima, totals, accumulated = running
    query_count = queries.shape[0]
    query_heads = queries.reshape(query_count, head_count, HD)
    key_heads = key_rows.reshape(key_rows.shape[0], head_count, HD)
    value_heads = value_part.reshape(value_part.shape[0], head_count, HD)
    scores = (
        jnp.einsum("qhd,khd->hqk", query_heads, key_heads, preferred_element_type=jnp.float32)
        * score_scale
    )
    allowed = (query_mark[:, None] == key_mark[None, :])[None]
    scores = jnp.where(allowed, scores, -1e30)
    new_max = jnp.maximum(maxima, jnp.max(scores, axis=2))
    factor = jnp.exp(maxima - new_max)
    weights = jnp.where(allowed, jnp.exp(scores - new_max[:, :, None]), 0.0)
    totals = totals * factor + jnp.sum(weights, axis=2)
    update = jnp.einsum(
        "hqk,khd->qhd",
        weights.astype(jnp.bfloat16),
        value_heads,
        preferred_element_type=jnp.float32,
    )
    accumulated = accumulated * jnp.transpose(factor)[:, :, None] + update
    return (new_max, totals, accumulated)


def attend_blocks(
    running, queries, query_mark, key_rows, value_part, key_mark, head_count, score_scale
):
    block_rows = queries.shape[0]
    block_count = key_rows.shape[0] // block_rows
    stacked = (
        key_rows.reshape(block_count, block_rows, key_rows.shape[1]),
        value_part.reshape(block_count, block_rows, value_part.shape[1]),
        key_mark.reshape(block_count, block_rows),
    )

    def advance(state, shard_piece):
        return (
            attend(
                state,
                queries,
                query_mark,
                shard_piece[0],
                shard_piece[1],
                shard_piece[2],
                head_count,
                score_scale,
            ),
            None,
        )

    running, unused = lax.scan(advance, running, stacked)
    return running


def general_local(
    query_raw,
    key_raw,
    value_rows,
    query_gain,
    key_gain,
    segment,
    destination,
    timestep,
    out_weight,
    gate_table,
):
    row_count = query_raw.shape[0]
    row_width = query_raw.shape[1]
    head_count = row_width // HD
    ctx_size = lax.axis_size("ctx")
    total_width = row_width * lax.axis_size("head")
    score_scale = 1.0 / math.sqrt(HD)
    query_float = query_raw.astype(jnp.float32)
    key_float = key_raw.astype(jnp.float32)
    query_sum, key_sum = lax.psum(
        (jnp.sum(query_float * query_float, axis=1), jnp.sum(key_float * key_float, axis=1)), "head"
    )
    queries = (
        query_float * lax.rsqrt(query_sum / total_width + 1e-06)[:, None] * query_gain
    ).astype(jnp.bfloat16)
    normed_keys = (key_float * lax.rsqrt(key_sum / total_width + 1e-06)[:, None] * key_gain).astype(
        jnp.bfloat16
    )
    slot_count = row_count // ctx_size
    target = destination // row_count * slot_count + destination % slot_count

    def placed(array):
        return jnp.zeros_like(array).at[target].set(array)

    initial = (
        jnp.full((head_count, row_count), -1e30, jnp.float32),
        jnp.zeros((head_count, row_count), jnp.float32),
        jnp.zeros((row_count, head_count, HD), jnp.float32),
    )
    own_queries, own_keys, own_values, own_segment = (
        lax.all_to_all(placed(queries), "ctx", split_axis=0, concat_axis=0, tiled=True),
        lax.all_to_all(placed(normed_keys), "ctx", split_axis=0, concat_axis=0, tiled=True),
        lax.all_to_all(placed(value_rows), "ctx", split_axis=0, concat_axis=0, tiled=True),
        lax.all_to_all(placed(segment), "ctx", split_axis=0, concat_axis=0, tiled=True),
    )
    running = attend_blocks(
        initial,
        own_queries,
        own_segment,
        lax.all_gather(own_keys, "ctx", axis=0, tiled=True),
        lax.all_gather(own_values, "ctx", axis=0, tiled=True),
        lax.all_gather(for_sending(own_segment), "ctx", axis=0, tiled=True),
        head_count,
        score_scale,
    )
    attended = (
        (running[2] / jnp.transpose(running[1])[:, :, None])
        .reshape(row_count, row_width)
        .astype(jnp.bfloat16)
    )
    head_terms = jnp.dot(attended, out_weight, preferred_element_type=jnp.float32)
    mixed_rows = lax.psum_scatter(
        head_terms.astype(jnp.bfloat16), "head", scatter_dimension=1, tiled=True
    ).astype(jnp.float32)
    video_gates = jnp.dot(
        jax.nn.one_hot(timestep, gate_table.shape[0], dtype=jnp.float32),
        gate_table,
        precision=lax.Precision.HIGHEST,
    )
    token_gates = jnp.dot(
        jax.nn.one_hot(own_segment, timestep.shape[0], dtype=jnp.float32),
        video_gates,
        precision=lax.Precision.HIGHEST,
    )
    return (mixed_rows * token_gates).astype(jnp.bfloat16)


def solution(mesh):
    placed = (
        P(("batch", "ctx"), "head"),
        P(("batch", "ctx"), "head"),
        P(("batch", "ctx"), "head"),
        P("head"),
        P("head"),
        P(("batch", "ctx")),
        P(("batch", "ctx")),
        P("batch"),
        P("head", None),
        P(None, "head"),
    )
    sizes = dict(mesh.shape)
    fast = sizes["batch"] == 4 and sizes["ctx"] == 2 and sizes["head"] == 4
    local = fast_local if fast else general_local
    return jax.shard_map(
        local, mesh=mesh, in_specs=placed, out_specs=P(("batch", "ctx"), "head"), check_vma=False
    )
```

```python
import functools
import math

import jax
import jax.numpy as jnp
from jax import lax
from jax.experimental import pallas as pl
from jax.experimental.pallas import tpu as pltpu
from jax.sharding import PartitionSpec as P

HD = 128
F32 = jnp.float32
BF16 = jnp.bfloat16
VMEM = pl.BlockSpec(memory_space=pltpu.VMEM)
SMEM = pl.BlockSpec(memory_space=pltpu.SMEM)
ANY = pl.BlockSpec(memory_space=pl.ANY)
HBM = pl.BlockSpec(memory_space=pltpu.HBM)
AFTER = VMEM
SENDS = (3, 2)

SWAP_CTX = ((0, 1), (1, 0))
SWAP_CORE = ((0, 1), (1, 0), (2, 3), (3, 2))
SWAP_X = ((0, 2), (2, 0), (1, 3), (3, 1))


def xor_pairs(size, step):
    return tuple((i, i ^ step) for i in range(size))


def params(mebibytes):
    return pltpu.CompilerParams(vmem_limit_bytes=mebibytes * 1024 * 1024)


def cost(microseconds):
    return pl.CostEstimate(flops=0, bytes_accessed=int(microseconds * 3_600_000), transcendentals=0)


def load(pairs, sems):
    copies = [pltpu.make_async_copy(source, target, sems.at[i]) for i, (source, target) in enumerate(pairs)]
    for copy in copies:
        copy.start()
    return copies


def row_sums(values):
    squares = values * values
    folded = squares[:, 0:HD]
    for low in range(HD, values.shape[1], HD):
        folded = folded + squares[:, low : low + HD]
    return jnp.sum(jnp.transpose(folded), axis=0, keepdims=True)


def three_pieces(value):
    pieces = []
    for _ in range(3):
        short = value.astype(BF16).astype(F32)
        pieces.append(short)
        value = value - short
    return pieces


def column(row):
    return jnp.transpose(jnp.broadcast_to(row, (8, row.shape[1])))[:, 0:1]


def prepare_kernel(
    cut, place, q_hbm, k_hbm, v_hbm, dest_hbm, seg_hbm, weight_ref,
    own_ref, other_ref, packed_ref, stats_ref, k_ref, v_ref, one_ref, two_ref, three_ref,
    q_ref, dest_ref, seg_ref, sems,
):
    pairs = [(dest_hbm, dest_ref), (seg_hbm, seg_ref), (q_hbm, q_ref), (k_hbm, k_ref), (v_hbm, v_ref)]
    for step, (ref, index) in enumerate(((one_ref, place[3]), (two_ref, place[2]), (three_ref, place[2]))):
        count, columns = ref.shape
        first = pl.multiple_of(index * count, count)
        start = pl.multiple_of((place[1] ^ (step + 1)) * columns, columns)
        pairs.append((weight_ref.at[pl.ds(first, count), pl.ds(start, columns)], ref))
    copies = load(pairs, sems)
    rows = q_ref.shape[0]
    half = rows // 2
    low, high = cut
    me = place[0]
    copies[0].wait()
    copies[1].wait()
    dest = dest_ref[...]
    block = (dest >= rows).astype(jnp.int32)
    slot = dest - block * rows - me * half + jnp.where(block == me, 0, half)
    spread = (lax.broadcasted_iota(jnp.int32, (rows, rows), 0) == slot).astype(BF16)
    marks = seg_ref[...].astype(F32)
    moved_marks = lax.dot_general(
        jnp.broadcast_to(marks, (8, rows)).astype(BF16), spread, (((1,), (1,)), ((), ())),
        preferred_element_type=F32,
    )[0:1]
    copies[2].wait()
    moved = jnp.dot(spread, q_ref[...], preferred_element_type=F32)
    moved_short = moved.astype(BF16)
    own_ref[...] = moved_short[:half]
    other_ref[...] = moved_short[half:]
    packed_ref[0:half, :] = moved_short[half:, low:high]
    query_sums = row_sums(moved)
    copies[3].wait()
    packed_ref[half : half + rows, :] = k_ref[:, low:high]
    key_sums = row_sums(k_ref[...].astype(F32))
    stats_ref[...] = jnp.concatenate(
        [query_sums, key_sums, moved_marks, marks, jnp.zeros((4, rows), F32)], axis=0
    )
    copies[4].wait()
    packed_ref[half + rows :, :] = v_ref[:, low:high]
    for copy in copies[5:]:
        copy.wait()


def settle_kernel(near_ref, far_ref, *refs):
    refs[-1][...] = near_ref[...] + far_ref[...]


def pack_kernel(cut, other_ref, k_ref, v_ref, after_ref, out_ref):
    low, high = cut
    half, rows = other_ref.shape[0], k_ref.shape[0]
    out_ref[0:half, :] = other_ref[:, low:high]
    out_ref[half : half + rows, :] = k_ref[:, low:high]
    out_ref[half + rows :, :] = v_ref[:, low:high]


def attend_kernel(
    cut, total_width, place, near_ref, far_ref, q_ref, k_ref, v_ref, qg_ref, kg_ref, remote_ref, *refs
):
    out_ref = refs[-1]
    rows = k_ref.shape[0]
    half = rows // 2
    me = place[0]
    near, far = near_ref[...], far_ref[...]
    near_factors = lax.rsqrt(near[0:2] / total_width + 1e-06)
    far_factors = lax.rsqrt(far[0:2] / total_width + 1e-06)
    q_mark = jnp.concatenate([near[2:3, :half], far[2:3, half:]], axis=1)
    k_mark = jnp.concatenate([near[3:4], far[3:4]], axis=1)
    q_factor = column(jnp.concatenate([near_factors[0:1, :half], far_factors[0:1, half:]], axis=1))
    k_factor = column(jnp.concatenate([near_factors[1:2], far_factors[1:2]], axis=1))
    allowed = column(q_mark) == k_mark
    scale = math.log2(math.e) / math.sqrt(HD)
    first, last = cut
    for low in range(first, last, HD):
        here = slice(low - first, low - first + HD)
        wide = slice(low, low + HD)
        queries = jnp.concatenate([q_ref[:, wide], remote_ref[0:half, here]], axis=0)
        keys = jnp.concatenate([k_ref[:, wide], remote_ref[half : half + rows, here]], axis=0)
        values = jnp.concatenate([v_ref[:, wide], remote_ref[half + rows :, here]], axis=0)
        queries = (queries.astype(F32) * q_factor * qg_ref[0:1, wide]).astype(BF16)
        keys = (keys.astype(F32) * k_factor * kg_ref[0:1, wide]).astype(BF16)
        for part in range(2):
            piece = slice(part * half, (part + 1) * half)
            scores = lax.dot_general(
                queries[piece], keys, (((1,), (1,)), ((), ())), preferred_element_type=F32
            )
            scores = jnp.where(allowed[piece], scores, -1e30)
            largest = jnp.max(scores, axis=1, keepdims=True)
            weights = jnp.exp2((scores - largest) * scale)
            totals = jnp.sum(weights, axis=1, keepdims=True)
            mixed = jnp.dot(weights.astype(BF16), values, preferred_element_type=F32)
            start = me * half if part == 0 else (1 - me) * half
            at = pl.ds(pl.multiple_of(start, half), half)
            out_ref[at, here] = (mixed / totals).astype(BF16)


def join_kernel(count, *refs):
    low = 0
    for ref in refs[:count]:
        refs[-1][low : low + ref.shape[0], :] = ref[...]
        low += ref.shape[0]


def join(pieces, after, name):
    return pl.pallas_call(
        functools.partial(join_kernel, len(pieces)),
        in_specs=[VMEM] * len(pieces) + [AFTER] * len(after),
        out_specs=VMEM,
        out_shape=jax.ShapeDtypeStruct((sum([piece.shape[0] for piece in pieces]), pieces[0].shape[1]), BF16),
        compiler_params=params(4),
        cost_estimate=cost(1),
        name=name,
    )(*pieces, *after)


def project_kernel(place, times, gate_ref, weight_ref, *refs):
    first, own_last, shares = refs[:4], refs[4], refs[5:13]
    total, tail_ref, gates_ref, rows_all, w_all, sems = refs[13:]
    width = total.shape[1]
    group = w_all.shape[1]
    share = group // 8
    early = first[0].shape[1]
    head, mine = place[1], place[2]
    own_start = pl.multiple_of(head * width, width)
    own_copy = pltpu.make_async_copy(weight_ref.at[:, pl.ds(own_start, width)], w_all.at[0], sems.at[0])
    own_copy.start()
    for slot in range(4):
        rows_all[:, slot * early : (slot + 1) * early] = first[slot][...]
    rows_all[:, 4 * early :] = own_last[...]
    gates_ref[...] = jnp.zeros(gates_ref.shape, BF16)
    for video in range(times.shape[0]):
        for index, piece in enumerate(three_pieces(gate_ref[pl.ds(times[video], 1), :])):
            gates_ref[index * 16 + video : index * 16 + video + 1, :] = piece.astype(BF16)
    for core in range(2):
        near, far, other, diagonal = shares[4 * core : 4 * core + 4]
        pieces = [(near, 0, 0, 0), (far, 0, 0, 4)]
        for step in (1, 2):
            pieces += [
                (near, (step + 1) * share, step, 0),
                (far, (step + 1) * share, step, 4),
                (other, (step - 1) * share, step, 1),
                (diagonal, (step - 1) * share, step, 5),
            ]
        for ref, low, step, flip in pieces:
            count = share if step else 2 * share
            index = mine ^ (flip + 2 * core) if step else place[3] ^ (flip // 2 + core)
            w_all[1 + step, pl.ds(pl.multiple_of(index * count, count), count), :] = ref[low : low + count, :]
    for step in range(3):
        tail_ref[step * (group - early) : (step + 1) * (group - early), :] = w_all[1 + step, early:group, :]
    own_copy.wait()
    for low in range(0, width, 256):
        block = slice(low, low + 256)
        mixed = jnp.dot(rows_all[:, 4 * early :], w_all[0, early:group, block], preferred_element_type=F32)
        for slot in range(4):
            mixed += jnp.dot(
                rows_all[:, slot * early : (slot + 1) * early], w_all[slot, 0:early, block],
                preferred_element_type=F32,
            )
        total[:, block] = mixed


def finish_kernel(place, near_ref, far_ref, total, tail_ref, gates_ref, one, two, three, out_hbm, out_ref, sems):
    rows, width = out_ref.shape
    half = rows // 2
    me = place[0]
    videos = lax.rem(lax.broadcasted_iota(jnp.int32, (rows, gates_ref.shape[0]), 1), 16).astype(F32)
    own_mark, other_mark = near_ref[2:3, :half], far_ref[2:3, half:]
    marks = jnp.concatenate(
        [jnp.where(me == 0, own_mark, other_mark), jnp.where(me == 0, other_mark, own_mark)], axis=1
    )
    picked = (column(marks) == 4.0 * videos).astype(BF16)
    late = jnp.concatenate([one[...], two[...], three[...]], axis=1)
    copies = []
    for index, low in enumerate(range(0, width, 256)):
        block = slice(low, low + 256)
        gates = jnp.dot(picked, gates_ref[:, block], preferred_element_type=F32)
        mixed = total[:, block] + jnp.dot(late, tail_ref[:, block], preferred_element_type=F32)
        out_ref[:, block] = (mixed * gates).astype(BF16)
        copies.append(pltpu.make_async_copy(out_ref.at[:, block], out_hbm.at[:, block], sems.at[index]))
        copies[-1].start()
    for copy in copies:
        copy.wait()


def fast_local(
    query_raw, key_raw, value_rows, query_gain, key_gain, segment, destination, timestep, out_weight, gate_table
):
    rows, width = query_raw.shape
    half = rows // 2
    out_width = gate_table.shape[1]
    total_width = width * lax.axis_size("head")
    ctx, head, batch = lax.axis_index("ctx"), lax.axis_index("head"), lax.axis_index("batch")
    mine = batch * 2 + ctx
    place = jnp.stack([ctx, head, mine, batch]).astype(jnp.int32)
    cuts, low = [], 0
    for count in SENDS:
        cuts.append((low * HD, (low + count) * HD))
        low += count
    assert low * HD == width
    share = width // 8
    packed_shapes = [jax.ShapeDtypeStruct((half + 2 * rows, high - low), BF16) for low, high in cuts]
    in_hbm = functools.partial(pltpu.with_memory_space_constraint, memory_space=pltpu.HBM)
    weight_hbm = in_hbm(out_weight)

    own_queries, other_queries, packed, stats, keys, values, *cut_weights = pl.pallas_call(
        functools.partial(prepare_kernel, cuts[0]),
        in_specs=[SMEM] + [HBM] * 6,
        out_specs=[VMEM] * 9,
        out_shape=[
            jax.ShapeDtypeStruct((half, width), BF16),
            jax.ShapeDtypeStruct((half, width), BF16),
            packed_shapes[0],
            jax.ShapeDtypeStruct((8, rows), F32),
            jax.ShapeDtypeStruct((rows, width), BF16),
            jax.ShapeDtypeStruct((rows, width), BF16),
            jax.ShapeDtypeStruct((2 * share, out_width), BF16),
            jax.ShapeDtypeStruct((share, out_width), BF16),
            jax.ShapeDtypeStruct((share, out_width), BF16),
        ],
        scratch_shapes=[
            pltpu.VMEM((rows, width), BF16),
            pltpu.VMEM((1, rows), jnp.int32),
            pltpu.VMEM((1, rows), jnp.int32),
            pltpu.SemaphoreType.DMA((8,)),
        ],
        compiler_params=params(16),
        cost_estimate=cost(2),
        name="prepare",
    )(
        place, in_hbm(query_raw), in_hbm(key_raw), in_hbm(value_rows),
        in_hbm(destination.reshape(1, rows)), in_hbm(segment.reshape(1, rows)), weight_hbm,
    )
    from_head = [lax.ppermute(cut_weights[s - 1], "head", xor_pairs(4, s)) for s in (1, 2, 3)]
    arrived = [lax.ppermute(packed, "ctx", SWAP_CTX)]
    stats = stats + lax.ppermute(stats, "head", xor_pairs(4, 1))
    near = pl.pallas_call(
        settle_kernel,
        in_specs=[VMEM] * 2 + [AFTER] * 4,
        out_specs=VMEM,
        out_shape=jax.ShapeDtypeStruct((8, rows), F32),
        compiler_params=params(4),
        cost_estimate=cost(1),
        name="settle",
    )(stats, lax.ppermute(stats, "head", xor_pairs(4, 2)), arrived[0], *from_head)
    far = lax.ppermute(near, "ctx", SWAP_CTX)

    two_three = join(from_head[1:], [far], "join_two")
    share0 = join(from_head, [two_three], "join_all")
    share_y = lax.ppermute(two_three, "ctx", SWAP_CTX)
    share_x = lax.ppermute(share0, "batch", SWAP_X)

    def attend(cut, piece, after):
        return pl.pallas_call(
            functools.partial(attend_kernel, cut, total_width),
            in_specs=[SMEM] + [VMEM] * 8 + [AFTER] * len(after),
            out_specs=VMEM,
            out_shape=jax.ShapeDtypeStruct((rows, cut[1] - cut[0]), BF16),
            compiler_params=params(14),
            cost_estimate=cost(8),
            name="attend",
        )(
            place, near, far, own_queries, keys, values, query_gain.reshape(1, width),
            key_gain.reshape(1, width), piece, *after,
        )

    def spread(attended):
        one = lax.ppermute(attended, "head", xor_pairs(4, 1))
        two = lax.ppermute(attended, "head", xor_pairs(4, 2))
        three = lax.ppermute(two, "head", xor_pairs(4, 1))
        return [attended, one, two, three]

    first = spread(attend(cuts[0], arrived[0], [share0]))
    packed = pl.pallas_call(
        functools.partial(pack_kernel, cuts[1]),
        in_specs=[VMEM] * 3 + [AFTER],
        out_specs=VMEM,
        out_shape=packed_shapes[1],
        compiler_params=params(4),
        cost_estimate=cost(1),
        name="pack",
    )(other_queries, keys, values, first[0])
    arrived.append(lax.ppermute(packed, "ctx", SWAP_CTX))
    share_y = join([share_y], first[1:3] + [packed], "hold")
    share_xy = lax.ppermute(share_y, "batch", SWAP_X)
    last = spread(attend(cuts[1], arrived[1], [share_y]))
    shares = [share0, share_x, share_y, share_xy]
    shares += [lax.ppermute(value, "batch", SWAP_CORE) for value in shares]

    tail = width - cuts[0][1]
    total, tail_weights, gates = pl.pallas_call(
        project_kernel,
        in_specs=[SMEM, SMEM, VMEM, HBM] + [VMEM] * 13,
        out_specs=[VMEM] * 3,
        out_shape=[
            jax.ShapeDtypeStruct((rows, out_width), F32),
            jax.ShapeDtypeStruct((3 * tail, out_width), BF16),
            jax.ShapeDtypeStruct((48, out_width), BF16),
        ],
        scratch_shapes=[
            pltpu.VMEM((rows, 3 * cuts[0][1] + width), BF16),
            pltpu.VMEM((4, width, out_width), BF16),
            pltpu.SemaphoreType.DMA((1,)),
        ],
        compiler_params=params(24),
        cost_estimate=cost(0),
        name="project",
    )(place, timestep, gate_table, weight_hbm, *first, last[0], *shares)
    return pl.pallas_call(
        finish_kernel,
        in_specs=[SMEM] + [VMEM] * 8,
        out_specs=ANY,
        out_shape=jax.ShapeDtypeStruct((rows, out_width), BF16),
        scratch_shapes=[
            pltpu.VMEM((rows, out_width), BF16),
            pltpu.SemaphoreType.DMA((out_width // 256,)),
        ],
        compiler_params=params(14),
        cost_estimate=cost(0),
        name="finish",
    )(place, near, far, total, tail_weights, gates, *last[1:])


def for_sending(array):

    def short(part):
        return part.astype(jnp.bfloat16) if part.dtype == jnp.float32 else part

    return jax.tree.map(short, array)


def attend(running, queries, query_mark, key_rows, value_part, key_mark, head_count, score_scale):
    maxima, totals, accumulated = running
    query_count = queries.shape[0]
    query_heads = queries.reshape(query_count, head_count, HD)
    key_heads = key_rows.reshape(key_rows.shape[0], head_count, HD)
    value_heads = value_part.reshape(value_part.shape[0], head_count, HD)
    scores = (
        jnp.einsum("qhd,khd->hqk", query_heads, key_heads, preferred_element_type=jnp.float32)
        * score_scale
    )
    allowed = (query_mark[:, None] == key_mark[None, :])[None]
    scores = jnp.where(allowed, scores, -1e30)
    new_max = jnp.maximum(maxima, jnp.max(scores, axis=2))
    factor = jnp.exp(maxima - new_max)
    weights = jnp.where(allowed, jnp.exp(scores - new_max[:, :, None]), 0.0)
    totals = totals * factor + jnp.sum(weights, axis=2)
    update = jnp.einsum(
        "hqk,khd->qhd",
        weights.astype(jnp.bfloat16),
        value_heads,
        preferred_element_type=jnp.float32,
    )
    accumulated = accumulated * jnp.transpose(factor)[:, :, None] + update
    return (new_max, totals, accumulated)


def attend_blocks(
    running, queries, query_mark, key_rows, value_part, key_mark, head_count, score_scale
):
    block_rows = queries.shape[0]
    block_count = key_rows.shape[0] // block_rows
    stacked = (
        key_rows.reshape(block_count, block_rows, key_rows.shape[1]),
        value_part.reshape(block_count, block_rows, value_part.shape[1]),
        key_mark.reshape(block_count, block_rows),
    )

    def advance(state, shard_piece):
        return (
            attend(
                state,
                queries,
                query_mark,
                shard_piece[0],
                shard_piece[1],
                shard_piece[2],
                head_count,
                score_scale,
            ),
            None,
        )

    running, unused = lax.scan(advance, running, stacked)
    return running


def general_local(
    query_raw,
    key_raw,
    value_rows,
    query_gain,
    key_gain,
    segment,
    destination,
    timestep,
    out_weight,
    gate_table,
):
    row_count = query_raw.shape[0]
    row_width = query_raw.shape[1]
    head_count = row_width // HD
    ctx_size = lax.axis_size("ctx")
    total_width = row_width * lax.axis_size("head")
    score_scale = 1.0 / math.sqrt(HD)
    query_float = query_raw.astype(jnp.float32)
    key_float = key_raw.astype(jnp.float32)
    query_sum, key_sum = lax.psum(
        (jnp.sum(query_float * query_float, axis=1), jnp.sum(key_float * key_float, axis=1)), "head"
    )
    queries = (
        query_float * lax.rsqrt(query_sum / total_width + 1e-06)[:, None] * query_gain
    ).astype(jnp.bfloat16)
    normed_keys = (key_float * lax.rsqrt(key_sum / total_width + 1e-06)[:, None] * key_gain).astype(
        jnp.bfloat16
    )
    slot_count = row_count // ctx_size
    target = destination // row_count * slot_count + destination % slot_count

    def placed(array):
        return jnp.zeros_like(array).at[target].set(array)

    initial = (
        jnp.full((head_count, row_count), -1e30, jnp.float32),
        jnp.zeros((head_count, row_count), jnp.float32),
        jnp.zeros((row_count, head_count, HD), jnp.float32),
    )
    own_queries, own_keys, own_values, own_segment = (
        lax.all_to_all(placed(queries), "ctx", split_axis=0, concat_axis=0, tiled=True),
        lax.all_to_all(placed(normed_keys), "ctx", split_axis=0, concat_axis=0, tiled=True),
        lax.all_to_all(placed(value_rows), "ctx", split_axis=0, concat_axis=0, tiled=True),
        lax.all_to_all(placed(segment), "ctx", split_axis=0, concat_axis=0, tiled=True),
    )
    running = attend_blocks(
        initial,
        own_queries,
        own_segment,
        lax.all_gather(own_keys, "ctx", axis=0, tiled=True),
        lax.all_gather(own_values, "ctx", axis=0, tiled=True),
        lax.all_gather(for_sending(own_segment), "ctx", axis=0, tiled=True),
        head_count,
        score_scale,
    )
    attended = (
        (running[2] / jnp.transpose(running[1])[:, :, None])
        .reshape(row_count, row_width)
        .astype(jnp.bfloat16)
    )
    head_terms = jnp.dot(attended, out_weight, preferred_element_type=jnp.float32)
    mixed_rows = lax.psum_scatter(
        head_terms.astype(jnp.bfloat16), "head", scatter_dimension=1, tiled=True
    ).astype(jnp.float32)
    video_gates = jnp.dot(
        jax.nn.one_hot(timestep, gate_table.shape[0], dtype=jnp.float32),
        gate_table,
        precision=lax.Precision.HIGHEST,
    )
    token_gates = jnp.dot(
        jax.nn.one_hot(own_segment, timestep.shape[0], dtype=jnp.float32),
        video_gates,
        precision=lax.Precision.HIGHEST,
    )
    return (mixed_rows * token_gates).astype(jnp.bfloat16)


def solution(mesh):
    placed = (
        P(("batch", "ctx"), "head"),
        P(("batch", "ctx"), "head"),
        P(("batch", "ctx"), "head"),
        P("head"),
        P("head"),
        P(("batch", "ctx")),
        P(("batch", "ctx")),
        P("batch"),
        P("head", None),
        P(None, "head"),
    )
    sizes = dict(mesh.shape)
    fast = sizes["batch"] == 4 and sizes["ctx"] == 2 and sizes["head"] == 4
    local = fast_local if fast else general_local
    return jax.shard_map(
        local, mesh=mesh, in_specs=placed, out_specs=P(("batch", "ctx"), "head"), check_vma=False
    )
```

```python
import functools
import math

import jax
import jax.numpy as jnp
from jax import lax
from jax.experimental import pallas as pl
from jax.experimental.pallas import tpu as pltpu
from jax.sharding import PartitionSpec as P

HD = 128
F32 = jnp.float32
BF16 = jnp.bfloat16
VMEM = pl.BlockSpec(memory_space=pltpu.VMEM)
SMEM = pl.BlockSpec(memory_space=pltpu.SMEM)
ANY = pl.BlockSpec(memory_space=pl.ANY)
HBM = pl.BlockSpec(memory_space=pltpu.HBM)
AFTER = VMEM
SENDS = (3, 2)

SWAP_CTX = ((0, 1), (1, 0))
SWAP_CORE = ((0, 1), (1, 0), (2, 3), (3, 2))
SWAP_X = ((0, 2), (2, 0), (1, 3), (3, 1))


def xor_pairs(size, step):
    return tuple((i, i ^ step) for i in range(size))


def params(mebibytes):
    return pltpu.CompilerParams(vmem_limit_bytes=mebibytes * 1024 * 1024)


def cost(microseconds):
    return pl.CostEstimate(flops=0, bytes_accessed=int(microseconds * 3_600_000), transcendentals=0)


def load(pairs, sems):
    copies = [pltpu.make_async_copy(source, target, sems.at[i]) for i, (source, target) in enumerate(pairs)]
    for copy in copies:
        copy.start()
    return copies


def row_sums(values):
    squares = values * values
    folded = squares[:, 0:HD]
    for low in range(HD, values.shape[1], HD):
        folded = folded + squares[:, low : low + HD]
    return jnp.sum(jnp.transpose(folded), axis=0, keepdims=True)


def three_pieces(value):
    pieces = []
    for _ in range(3):
        short = value.astype(BF16).astype(F32)
        pieces.append(short)
        value = value - short
    return pieces


def column(row):
    return jnp.transpose(jnp.broadcast_to(row, (8, row.shape[1])))[:, 0:1]


def prepare_kernel(
    cut, place, q_hbm, k_hbm, v_hbm, dest_hbm, seg_hbm,
    own_ref, other_ref, packed_ref, stats_ref, k_ref, v_ref,
    q_ref, dest_ref, seg_ref, sems,
):
    pairs = [(dest_hbm, dest_ref), (seg_hbm, seg_ref), (q_hbm, q_ref), (k_hbm, k_ref), (v_hbm, v_ref)]
    copies = load(pairs, sems)
    rows = q_ref.shape[0]
    half = rows // 2
    low, high = cut
    me = place[0]
    copies[0].wait()
    copies[1].wait()
    dest = dest_ref[...]
    block = (dest >= rows).astype(jnp.int32)
    slot = dest - block * rows - me * half + jnp.where(block == me, 0, half)
    spread = (lax.broadcasted_iota(jnp.int32, (rows, rows), 0) == slot).astype(BF16)
    marks = seg_ref[...].astype(F32)
    moved_marks = lax.dot_general(
        jnp.broadcast_to(marks, (8, rows)).astype(BF16), spread, (((1,), (1,)), ((), ())),
        preferred_element_type=F32,
    )[0:1]
    copies[2].wait()
    moved = jnp.dot(spread, q_ref[...], preferred_element_type=F32)
    moved_short = moved.astype(BF16)
    own_ref[...] = moved_short[:half]
    other_ref[...] = moved_short[half:]
    packed_ref[0:half, :] = moved_short[half:, low:high]
    query_sums = row_sums(moved)
    copies[3].wait()
    packed_ref[half : half + rows, :] = k_ref[:, low:high]
    key_sums = row_sums(k_ref[...].astype(F32))
    stats_ref[...] = jnp.concatenate(
        [query_sums, key_sums, moved_marks, marks, jnp.zeros((4, rows), F32)], axis=0
    )
    copies[4].wait()
    packed_ref[half + rows :, :] = v_ref[:, low:high]


def settle_kernel(near_ref, far_ref, out_ref):
    out_ref[...] = near_ref[...] + far_ref[...]


def cut_kernel(place, weight_ref, after_ref, one_ref, two_ref, three_ref, sems):
    pairs = []
    for step, (ref, index) in enumerate(((one_ref, place[3]), (two_ref, place[2]), (three_ref, place[2]))):
        count, columns = ref.shape
        first = pl.multiple_of(index * count, count)
        start = pl.multiple_of((place[1] ^ (step + 1)) * columns, columns)
        pairs.append((weight_ref.at[pl.ds(first, count), pl.ds(start, columns)], ref))
    for copy in load(pairs, sems):
        copy.wait()


def pack_kernel(cut, other_ref, k_ref, v_ref, *refs):
    out_ref = refs[-1]
    low, high = cut
    half, rows = other_ref.shape[0], k_ref.shape[0]
    out_ref[0:half, :] = other_ref[:, low:high]
    out_ref[half : half + rows, :] = k_ref[:, low:high]
    out_ref[half + rows :, :] = v_ref[:, low:high]


def attend_kernel(
    cut, total_width, place, near_ref, far_ref, q_ref, k_ref, v_ref, qg_ref, kg_ref, remote_ref, *refs
):
    out_ref = refs[-1]
    rows = k_ref.shape[0]
    half = rows // 2
    me = place[0]
    near, far = near_ref[...], far_ref[...]
    near_factors = lax.rsqrt(near[0:2] / total_width + 1e-06)
    far_factors = lax.rsqrt(far[0:2] / total_width + 1e-06)
    q_mark = jnp.concatenate([near[2:3, :half], far[2:3, half:]], axis=1)
    k_mark = jnp.concatenate([near[3:4], far[3:4]], axis=1)
    q_factor = column(jnp.concatenate([near_factors[0:1, :half], far_factors[0:1, half:]], axis=1))
    k_factor = column(jnp.concatenate([near_factors[1:2], far_factors[1:2]], axis=1))
    lane_video = 4.0 * lax.broadcasted_iota(jnp.int32, (2 * rows, HD), 1).astype(F32)
    q_video = jnp.where(column(q_mark) == lane_video[:rows], 1.0, 0.0).astype(BF16)
    k_video = jnp.where(column(k_mark) == lane_video, 0.0, -(2.0**20)).astype(BF16)
    ones = jnp.ones((2 * rows, HD), BF16)
    scale = math.log2(math.e) / math.sqrt(HD)
    first, last = cut
    for low in range(first, last, HD):
        here = slice(low - first, low - first + HD)
        wide = slice(low, low + HD)
        queries = jnp.concatenate([q_ref[:, wide], remote_ref[0:half, here]], axis=0)
        keys = jnp.concatenate([k_ref[:, wide], remote_ref[half : half + rows, here]], axis=0)
        values = jnp.concatenate([v_ref[:, wide], remote_ref[half + rows :, here]], axis=0)
        queries = (queries.astype(F32) * q_factor * qg_ref[0:1, wide]).astype(BF16)
        keys = (keys.astype(F32) * k_factor * kg_ref[0:1, wide]).astype(BF16)
        queries = jnp.concatenate([queries, q_video], axis=1)
        keys = jnp.concatenate([keys, k_video], axis=1)
        values = jnp.concatenate([values, ones], axis=1)
        for part in range(2):
            piece = slice(part * half, (part + 1) * half)
            scores = lax.dot_general(
                queries[piece], keys, (((1,), (1,)), ((), ())), preferred_element_type=F32
            )
            largest = jnp.max(scores, axis=1, keepdims=True)
            weights = jnp.exp2((scores - largest) * scale).astype(BF16)
            mixed = jnp.dot(weights, values, preferred_element_type=F32)
            mixed, totals = mixed[:, :HD], mixed[:, HD:]
            start = me * half if part == 0 else (1 - me) * half
            at = pl.ds(pl.multiple_of(start, half), half)
            out_ref[at, here] = (mixed / totals).astype(BF16)


def join_kernel(count, *refs):
    low = 0
    for ref in refs[:count]:
        refs[-1][low : low + ref.shape[0], :] = ref[...]
        low += ref.shape[0]


def gate_kernel(*refs):
    refs[-1][...] = jnp.zeros(refs[-1].shape, F32)


def gate(after, weight, name):
    return pl.pallas_call(
        gate_kernel,
        in_specs=[AFTER] * len(after),
        out_specs=VMEM,
        out_shape=jax.ShapeDtypeStruct((8, 128), F32),
        compiler_params=params(4),
        cost_estimate=pl.CostEstimate(flops=weight * 900_000_000, bytes_accessed=4096, transcendentals=0),
        name=name,
    )(*after)


def join(pieces, after, name):
    return pl.pallas_call(
        functools.partial(join_kernel, len(pieces)),
        in_specs=[VMEM] * len(pieces) + [AFTER] * len(after),
        out_specs=VMEM,
        out_shape=jax.ShapeDtypeStruct((sum([piece.shape[0] for piece in pieces]), pieces[0].shape[1]), BF16),
        compiler_params=params(4),
        cost_estimate=cost(1),
        name=name,
    )(*pieces, *after)


def project_kernel(place, times, gate_ref, weight_ref, *refs):
    first, own_last, shares = refs[:4], refs[4], refs[5:11]
    total, tail_ref, gates_ref, rows_all, w_all, sems = refs[11:]
    width = total.shape[1]
    group = w_all.shape[1]
    share = group // 8
    early = first[0].shape[1]
    head, mine = place[1], place[2]
    own_start = pl.multiple_of(head * width, width)
    own_copy = pltpu.make_async_copy(weight_ref.at[:, pl.ds(own_start, width)], w_all.at[0], sems.at[0])
    own_copy.start()
    for slot in range(4):
        rows_all[:, slot * early : (slot + 1) * early] = first[slot][...]
    rows_all[:, 4 * early :] = own_last[...]
    gates_ref[...] = jnp.zeros(gates_ref.shape, BF16)
    for video in range(times.shape[0]):
        for index, piece in enumerate(three_pieces(gate_ref[pl.ds(times[video], 1), :])):
            gates_ref[index * 16 + video : index * 16 + video + 1, :] = piece.astype(BF16)
    for core in range(2):
        near, far, other = shares[3 * core : 3 * core + 3]
        pieces = [(near, 0, 0, 0), (far, 0, 0, 4)]
        for step in (1, 2):
            pieces += [
                (near, (step + 1) * share, step, 0),
                (far, (step + 1) * share, step, 4),
                (other, (step - 1) * share, step, 1),
                (other, (step + 1) * share, step, 5),
            ]
        for ref, low, step, flip in pieces:
            count = share if step else 2 * share
            index = mine ^ (flip + 2 * core) if step else place[3] ^ (flip // 2 + core)
            w_all[1 + step, pl.ds(pl.multiple_of(index * count, count), count), :] = ref[low : low + count, :]
    for step in range(3):
        tail_ref[step * (group - early) : (step + 1) * (group - early), :] = w_all[1 + step, early:group, :]
    own_copy.wait()
    for low in range(0, width, 256):
        block = slice(low, low + 256)
        mixed = jnp.dot(rows_all[:, 4 * early :], w_all[0, early:group, block], preferred_element_type=F32)
        for slot in range(4):
            mixed += jnp.dot(
                rows_all[:, slot * early : (slot + 1) * early], w_all[slot, 0:early, block],
                preferred_element_type=F32,
            )
        total[:, block] = mixed


def finish_kernel(place, near_ref, far_ref, total, tail_ref, gates_ref, one, two, three, out_hbm, out_ref, sems):
    rows, width = out_ref.shape
    half = rows // 2
    me = place[0]
    videos = lax.rem(lax.broadcasted_iota(jnp.int32, (rows, gates_ref.shape[0]), 1), 16).astype(F32)
    own_mark, other_mark = near_ref[2:3, :half], far_ref[2:3, half:]
    marks = jnp.concatenate(
        [jnp.where(me == 0, own_mark, other_mark), jnp.where(me == 0, other_mark, own_mark)], axis=1
    )
    picked = (column(marks) == 4.0 * videos).astype(BF16)
    late = jnp.concatenate([one[...], two[...], three[...]], axis=1)
    copies = []
    for index, low in enumerate(range(0, width, 256)):
        block = slice(low, low + 256)
        gates = jnp.dot(picked, gates_ref[:, block], preferred_element_type=F32)
        mixed = total[:, block] + jnp.dot(late, tail_ref[:, block], preferred_element_type=F32)
        out_ref[:, block] = (mixed * gates).astype(BF16)
        copies.append(pltpu.make_async_copy(out_ref.at[:, block], out_hbm.at[:, block], sems.at[index]))
        copies[-1].start()
    for copy in copies:
        copy.wait()


def fast_local(
    query_raw, key_raw, value_rows, query_gain, key_gain, segment, destination, timestep, out_weight, gate_table
):
    rows, width = query_raw.shape
    half = rows // 2
    out_width = gate_table.shape[1]
    total_width = width * lax.axis_size("head")
    ctx, head, batch = lax.axis_index("ctx"), lax.axis_index("head"), lax.axis_index("batch")
    mine = batch * 2 + ctx
    place = jnp.stack([ctx, head, mine, batch]).astype(jnp.int32)
    cuts, low = [], 0
    for count in SENDS:
        cuts.append((low * HD, (low + count) * HD))
        low += count
    assert low * HD == width
    share = width // 8
    packed_shapes = [jax.ShapeDtypeStruct((half + 2 * rows, high - low), BF16) for low, high in cuts]
    in_hbm = functools.partial(pltpu.with_memory_space_constraint, memory_space=pltpu.HBM)
    weight_hbm = in_hbm(out_weight)

    own_queries, other_queries, packed, stats, keys, values = pl.pallas_call(
        functools.partial(prepare_kernel, cuts[0]),
        in_specs=[SMEM] + [HBM] * 5,
        out_specs=[VMEM] * 6,
        out_shape=[
            jax.ShapeDtypeStruct((half, width), BF16),
            jax.ShapeDtypeStruct((half, width), BF16),
            packed_shapes[0],
            jax.ShapeDtypeStruct((8, rows), F32),
            jax.ShapeDtypeStruct((rows, width), BF16),
            jax.ShapeDtypeStruct((rows, width), BF16),
        ],
        scratch_shapes=[
            pltpu.VMEM((rows, width), BF16),
            pltpu.VMEM((1, rows), jnp.int32),
            pltpu.VMEM((1, rows), jnp.int32),
            pltpu.SemaphoreType.DMA((5,)),
        ],
        compiler_params=params(16),
        cost_estimate=cost(2),
        name="prepare",
    )(
        place, in_hbm(query_raw), in_hbm(key_raw), in_hbm(value_rows),
        in_hbm(destination.reshape(1, rows)), in_hbm(segment.reshape(1, rows)),
    )
    arrived = [lax.ppermute(packed, "ctx", SWAP_CTX)]
    stats = stats + lax.ppermute(stats, "head", xor_pairs(4, 1))
    near = pl.pallas_call(
        settle_kernel,
        in_specs=[VMEM] * 2,
        out_specs=VMEM,
        out_shape=jax.ShapeDtypeStruct((8, rows), F32),
        compiler_params=params(4),
        cost_estimate=cost(1),
        name="settle",
    )(stats, lax.ppermute(stats, "head", xor_pairs(4, 2)))
    far = lax.ppermute(near, "ctx", SWAP_CTX)

    cut_weights = pl.pallas_call(
        cut_kernel,
        in_specs=[SMEM, HBM, AFTER],
        out_specs=[VMEM] * 3,
        out_shape=[jax.ShapeDtypeStruct((count * share, out_width), BF16) for count in (2, 1, 1)],
        scratch_shapes=[pltpu.SemaphoreType.DMA((3,))],
        compiler_params=params(4),
        cost_estimate=cost(1),
        name="cut_weights",
    )(place, weight_hbm, near)
    from_head = [lax.ppermute(cut_weights[s - 1], "head", xor_pairs(4, s)) for s in (1, 2, 3)]

    def attend(cut, piece, after):
        return pl.pallas_call(
            functools.partial(attend_kernel, cut, total_width),
            in_specs=[SMEM] + [VMEM] * 8 + [AFTER] * len(after),
            out_specs=VMEM,
            out_shape=jax.ShapeDtypeStruct((rows, cut[1] - cut[0]), BF16),
            compiler_params=params(14),
            cost_estimate=cost(8),
            name="attend",
        )(
            place, near, far, own_queries, keys, values, query_gain.reshape(1, width),
            key_gain.reshape(1, width), piece, *after,
        )

    def spread(attended):
        one = lax.ppermute(attended, "head", xor_pairs(4, 1))
        two = lax.ppermute(attended, "head", xor_pairs(4, 2))
        three = lax.ppermute(two, "head", xor_pairs(4, 1))
        return [attended, one, two, three]

    first = spread(attend(cuts[0], arrived[0], []))
    landed = gate(from_head, 10, "landed")
    packed = pl.pallas_call(
        functools.partial(pack_kernel, cuts[1]),
        in_specs=[VMEM] * 3 + [AFTER] * 2,
        out_specs=VMEM,
        out_shape=packed_shapes[1],
        compiler_params=params(4),
        cost_estimate=cost(1),
        name="pack",
    )(other_queries, keys, values, first[0], landed)
    arrived.append(lax.ppermute(packed, "ctx", SWAP_CTX))
    two_three = join(from_head[1:], [packed], "join_two")
    share0 = join(from_head, [packed], "join_all")
    share_y = lax.ppermute(two_three, "ctx", SWAP_CTX)
    share_x = lax.ppermute(share0, "batch", SWAP_X)

    token = gate(first[1:3], 10, "token")
    attended = attend(cuts[1], arrived[1], [token])
    share_y = join([share_y], [attended, share_x], "hold")
    share_xy = lax.ppermute(share_y, "batch", SWAP_X)
    last = spread(attended)
    passed = gate([first[3], *last[1:3]], 10, "passed")
    share_yxy = join([share_y, share_xy], [passed], "join_y")
    shares = [share0, share_x, share_yxy]
    shares += [lax.ppermute(value, "batch", SWAP_CORE) for value in shares]

    tail = width - cuts[0][1]
    total, tail_weights, gates = pl.pallas_call(
        project_kernel,
        in_specs=[SMEM, SMEM, VMEM, HBM] + [VMEM] * 11,
        out_specs=[VMEM] * 3,
        out_shape=[
            jax.ShapeDtypeStruct((rows, out_width), F32),
            jax.ShapeDtypeStruct((3 * tail, out_width), BF16),
            jax.ShapeDtypeStruct((48, out_width), BF16),
        ],
        scratch_shapes=[
            pltpu.VMEM((rows, 3 * cuts[0][1] + width), BF16),
            pltpu.VMEM((4, width, out_width), BF16),
            pltpu.SemaphoreType.DMA((1,)),
        ],
        compiler_params=params(24),
        cost_estimate=cost(0),
        name="project",
    )(place, timestep, gate_table, weight_hbm, *first, last[0], *shares)
    return pl.pallas_call(
        finish_kernel,
        in_specs=[SMEM] + [VMEM] * 8,
        out_specs=ANY,
        out_shape=jax.ShapeDtypeStruct((rows, out_width), BF16),
        scratch_shapes=[
            pltpu.VMEM((rows, out_width), BF16),
            pltpu.SemaphoreType.DMA((out_width // 256,)),
        ],
        compiler_params=params(14),
        cost_estimate=cost(0),
        name="finish",
    )(place, near, far, total, tail_weights, gates, *last[1:])


def for_sending(array):

    def short(part):
        return part.astype(jnp.bfloat16) if part.dtype == jnp.float32 else part

    return jax.tree.map(short, array)


def attend(running, queries, query_mark, key_rows, value_part, key_mark, head_count, score_scale):
    maxima, totals, accumulated = running
    query_count = queries.shape[0]
    query_heads = queries.reshape(query_count, head_count, HD)
    key_heads = key_rows.reshape(key_rows.shape[0], head_count, HD)
    value_heads = value_part.reshape(value_part.shape[0], head_count, HD)
    scores = (
        jnp.einsum("qhd,khd->hqk", query_heads, key_heads, preferred_element_type=jnp.float32)
        * score_scale
    )
    allowed = (query_mark[:, None] == key_mark[None, :])[None]
    scores = jnp.where(allowed, scores, -1e30)
    new_max = jnp.maximum(maxima, jnp.max(scores, axis=2))
    factor = jnp.exp(maxima - new_max)
    weights = jnp.where(allowed, jnp.exp(scores - new_max[:, :, None]), 0.0)
    totals = totals * factor + jnp.sum(weights, axis=2)
    update = jnp.einsum(
        "hqk,khd->qhd",
        weights.astype(jnp.bfloat16),
        value_heads,
        preferred_element_type=jnp.float32,
    )
    accumulated = accumulated * jnp.transpose(factor)[:, :, None] + update
    return (new_max, totals, accumulated)


def attend_blocks(
    running, queries, query_mark, key_rows, value_part, key_mark, head_count, score_scale
):
    block_rows = queries.shape[0]
    block_count = key_rows.shape[0] // block_rows
    stacked = (
        key_rows.reshape(block_count, block_rows, key_rows.shape[1]),
        value_part.reshape(block_count, block_rows, value_part.shape[1]),
        key_mark.reshape(block_count, block_rows),
    )

    def advance(state, shard_piece):
        return (
            attend(
                state,
                queries,
                query_mark,
                shard_piece[0],
                shard_piece[1],
                shard_piece[2],
                head_count,
                score_scale,
            ),
            None,
        )

    running, unused = lax.scan(advance, running, stacked)
    return running


def general_local(
    query_raw,
    key_raw,
    value_rows,
    query_gain,
    key_gain,
    segment,
    destination,
    timestep,
    out_weight,
    gate_table,
):
    row_count = query_raw.shape[0]
    row_width = query_raw.shape[1]
    head_count = row_width // HD
    ctx_size = lax.axis_size("ctx")
    total_width = row_width * lax.axis_size("head")
    score_scale = 1.0 / math.sqrt(HD)
    query_float = query_raw.astype(jnp.float32)
    key_float = key_raw.astype(jnp.float32)
    query_sum, key_sum = lax.psum(
        (jnp.sum(query_float * query_float, axis=1), jnp.sum(key_float * key_float, axis=1)), "head"
    )
    queries = (
        query_float * lax.rsqrt(query_sum / total_width + 1e-06)[:, None] * query_gain
    ).astype(jnp.bfloat16)
    normed_keys = (key_float * lax.rsqrt(key_sum / total_width + 1e-06)[:, None] * key_gain).astype(
        jnp.bfloat16
    )
    slot_count = row_count // ctx_size
    target = destination // row_count * slot_count + destination % slot_count

    def placed(array):
        return jnp.zeros_like(array).at[target].set(array)

    initial = (
        jnp.full((head_count, row_count), -1e30, jnp.float32),
        jnp.zeros((head_count, row_count), jnp.float32),
        jnp.zeros((row_count, head_count, HD), jnp.float32),
    )
    own_queries, own_keys, own_values, own_segment = (
        lax.all_to_all(placed(queries), "ctx", split_axis=0, concat_axis=0, tiled=True),
        lax.all_to_all(placed(normed_keys), "ctx", split_axis=0, concat_axis=0, tiled=True),
        lax.all_to_all(placed(value_rows), "ctx", split_axis=0, concat_axis=0, tiled=True),
        lax.all_to_all(placed(segment), "ctx", split_axis=0, concat_axis=0, tiled=True),
    )
    running = attend_blocks(
        initial,
        own_queries,
        own_segment,
        lax.all_gather(own_keys, "ctx", axis=0, tiled=True),
        lax.all_gather(own_values, "ctx", axis=0, tiled=True),
        lax.all_gather(for_sending(own_segment), "ctx", axis=0, tiled=True),
        head_count,
        score_scale,
    )
    attended = (
        (running[2] / jnp.transpose(running[1])[:, :, None])
        .reshape(row_count, row_width)
        .astype(jnp.bfloat16)
    )
    head_terms = jnp.dot(attended, out_weight, preferred_element_type=jnp.float32)
    mixed_rows = lax.psum_scatter(
        head_terms.astype(jnp.bfloat16), "head", scatter_dimension=1, tiled=True
    ).astype(jnp.float32)
    video_gates = jnp.dot(
        jax.nn.one_hot(timestep, gate_table.shape[0], dtype=jnp.float32),
        gate_table,
        precision=lax.Precision.HIGHEST,
    )
    token_gates = jnp.dot(
        jax.nn.one_hot(own_segment, timestep.shape[0], dtype=jnp.float32),
        video_gates,
        precision=lax.Precision.HIGHEST,
    )
    return (mixed_rows * token_gates).astype(jnp.bfloat16)


def solution(mesh):
    placed = (
        P(("batch", "ctx"), "head"),
        P(("batch", "ctx"), "head"),
        P(("batch", "ctx"), "head"),
        P("head"),
        P("head"),
        P(("batch", "ctx")),
        P(("batch", "ctx")),
        P("batch"),
        P("head", None),
        P(None, "head"),
    )
    sizes = dict(mesh.shape)
    fast = sizes["batch"] == 4 and sizes["ctx"] == 2 and sizes["head"] == 4
    local = fast_local if fast else general_local
    return jax.shard_map(
        local, mesh=mesh, in_specs=placed, out_specs=P(("batch", "ctx"), "head"), check_vma=False
    )
```

```python
import functools
import math

import jax
import jax.numpy as jnp
from jax import lax
from jax.experimental import pallas as pl
from jax.experimental.pallas import tpu as pltpu
from jax.sharding import PartitionSpec as P

HD = 128
F32 = jnp.float32
BF16 = jnp.bfloat16
VMEM = pl.BlockSpec(memory_space=pltpu.VMEM)
SMEM = pl.BlockSpec(memory_space=pltpu.SMEM)
ANY = pl.BlockSpec(memory_space=pl.ANY)
HBM = pl.BlockSpec(memory_space=pltpu.HBM)
AFTER = VMEM
SENDS = (3, 2)

SWAP_CTX = ((0, 1), (1, 0))
SWAP_CORE = ((0, 1), (1, 0), (2, 3), (3, 2))
SWAP_X = ((0, 2), (2, 0), (1, 3), (3, 1))


def xor_pairs(size, step):
    return tuple((i, i ^ step) for i in range(size))


def params(mebibytes):
    return pltpu.CompilerParams(vmem_limit_bytes=mebibytes * 1024 * 1024)


def cost(microseconds):
    return pl.CostEstimate(flops=0, bytes_accessed=int(microseconds * 3_600_000), transcendentals=0)


def load(pairs, sems):
    copies = [pltpu.make_async_copy(source, target, sems.at[i]) for i, (source, target) in enumerate(pairs)]
    for copy in copies:
        copy.start()
    return copies


def row_sums(values):
    squares = values * values
    folded = squares[:, 0:HD]
    for low in range(HD, values.shape[1], HD):
        folded = folded + squares[:, low : low + HD]
    return jnp.sum(jnp.transpose(folded), axis=0, keepdims=True)


def three_pieces(value):
    pieces = []
    for _ in range(3):
        short = value.astype(BF16).astype(F32)
        pieces.append(short)
        value = value - short
    return pieces


def column(row):
    return jnp.transpose(jnp.broadcast_to(row, (8, row.shape[1])))[:, 0:1]


def prepare_kernel(
    cut, place, q_hbm, k_hbm, v_hbm, dest_hbm, seg_hbm, weight_ref,
    own_ref, other_ref, packed_ref, stats_ref, k_ref, v_ref, one_ref, two_ref, three_ref,
    q_ref, dest_ref, seg_ref, sems,
):
    pairs = [(dest_hbm, dest_ref), (seg_hbm, seg_ref), (q_hbm, q_ref), (k_hbm, k_ref), (v_hbm, v_ref)]
    for step, (ref, index) in enumerate(((one_ref, place[3]), (two_ref, place[2]), (three_ref, place[2]))):
        count, columns = ref.shape
        first = pl.multiple_of(index * count, count)
        start = pl.multiple_of((place[1] ^ (step + 1)) * columns, columns)
        pairs.append((weight_ref.at[pl.ds(first, count), pl.ds(start, columns)], ref))
    copies = load(pairs, sems)
    rows = q_ref.shape[0]
    half = rows // 2
    low, high = cut
    me = place[0]
    copies[0].wait()
    copies[1].wait()
    dest = dest_ref[...]
    block = (dest >= rows).astype(jnp.int32)
    slot = dest - block * rows - me * half + jnp.where(block == me, 0, half)
    spread = (lax.broadcasted_iota(jnp.int32, (rows, rows), 0) == slot).astype(BF16)
    marks = seg_ref[...].astype(F32)
    moved_marks = lax.dot_general(
        jnp.broadcast_to(marks, (8, rows)).astype(BF16), spread, (((1,), (1,)), ((), ())),
        preferred_element_type=F32,
    )[0:1]
    copies[2].wait()
    moved = jnp.dot(spread, q_ref[...], preferred_element_type=F32)
    moved_short = moved.astype(BF16)
    own_ref[...] = moved_short[:half]
    other_ref[...] = moved_short[half:]
    packed_ref[0:half, :] = moved_short[half:, low:high]
    query_sums = row_sums(moved)
    copies[3].wait()
    packed_ref[half : half + rows, :] = k_ref[:, low:high]
    key_sums = row_sums(k_ref[...].astype(F32))
    stats_ref[...] = jnp.concatenate(
        [query_sums, key_sums, moved_marks, marks, jnp.zeros((4, rows), F32)], axis=0
    )
    copies[4].wait()
    packed_ref[half + rows :, :] = v_ref[:, low:high]
    for copy in copies[5:]:
        copy.wait()


def settle_kernel(own_ref, one_ref, two_ref, three_ref, out_ref):
    out_ref[...] = (own_ref[...] + one_ref[...]) + (two_ref[...] + three_ref[...])


def pack_kernel(cut, other_ref, k_ref, v_ref, *refs):
    out_ref = refs[-1]
    low, high = cut
    half, rows = other_ref.shape[0], k_ref.shape[0]
    out_ref[0:half, :] = other_ref[:, low:high]
    out_ref[half : half + rows, :] = k_ref[:, low:high]
    out_ref[half + rows :, :] = v_ref[:, low:high]


def attend_kernel(
    cut, total_width, near_ref, far_ref, q_ref, k_ref, v_ref, qg_ref, kg_ref, remote_ref, *refs
):
    out_ref = refs[-1]
    rows = k_ref.shape[0]
    half = rows // 2
    near, far = near_ref[...], far_ref[...]
    near_factors = lax.rsqrt(near[0:2] / total_width + 1e-06)
    far_factors = lax.rsqrt(far[0:2] / total_width + 1e-06)
    q_mark = jnp.concatenate([near[2:3, :half], far[2:3, half:]], axis=1)
    k_mark = jnp.concatenate([near[3:4], far[3:4]], axis=1)
    q_factor = column(jnp.concatenate([near_factors[0:1, :half], far_factors[0:1, half:]], axis=1))
    k_factor = column(jnp.concatenate([near_factors[1:2], far_factors[1:2]], axis=1))
    lane_video = 4.0 * lax.broadcasted_iota(jnp.int32, (2 * rows, HD), 1).astype(F32)
    q_video = jnp.where(column(q_mark) == lane_video[:rows], 1.0, 0.0).astype(BF16)
    k_video = jnp.where(column(k_mark) == lane_video, 0.0, -(2.0**20)).astype(BF16)
    ones = jnp.ones((2 * rows, HD), BF16)
    scale = math.log2(math.e) / math.sqrt(HD)
    first, last = cut
    for low in range(first, last, HD):
        here = slice(low - first, low - first + HD)
        wide = slice(low, low + HD)
        queries = jnp.concatenate([q_ref[:, wide], remote_ref[0:half, here]], axis=0)
        keys = jnp.concatenate([k_ref[:, wide], remote_ref[half : half + rows, here]], axis=0)
        values = jnp.concatenate([v_ref[:, wide], remote_ref[half + rows :, here]], axis=0)
        queries = (queries.astype(F32) * q_factor * qg_ref[0:1, wide]).astype(BF16)
        keys = (keys.astype(F32) * k_factor * kg_ref[0:1, wide]).astype(BF16)
        queries = jnp.concatenate([queries, q_video], axis=1)
        keys = jnp.concatenate([keys, k_video], axis=1)
        values = jnp.concatenate([values, ones], axis=1)
        for part in range(2):
            piece = slice(part * half, (part + 1) * half)
            scores = lax.dot_general(
                queries[piece], keys, (((1,), (1,)), ((), ())), preferred_element_type=F32
            )
            largest = jnp.max(scores, axis=1, keepdims=True)
            weights = jnp.exp2((scores - largest) * scale).astype(BF16)
            mixed = jnp.dot(weights, values, preferred_element_type=F32)
            mixed, totals = mixed[:, :HD], mixed[:, HD:]
            out_ref[piece, here] = (mixed / totals).astype(BF16)


def join_kernel(count, *refs):
    low = 0
    for ref in refs[:count]:
        refs[-1][low : low + ref.shape[0], :] = ref[...]
        low += ref.shape[0]


def gate_kernel(*refs):
    refs[-1][...] = jnp.zeros(refs[-1].shape, F32)


def gate(after, weight, name):
    return pl.pallas_call(
        gate_kernel,
        in_specs=[AFTER] * len(after),
        out_specs=VMEM,
        out_shape=jax.ShapeDtypeStruct((8, 128), F32),
        compiler_params=params(4),
        cost_estimate=pl.CostEstimate(flops=weight * 900_000_000, bytes_accessed=4096, transcendentals=0),
        name=name,
    )(*after)


def join(pieces, after, name):
    return pl.pallas_call(
        functools.partial(join_kernel, len(pieces)),
        in_specs=[VMEM] * len(pieces) + [AFTER] * len(after),
        out_specs=VMEM,
        out_shape=jax.ShapeDtypeStruct((sum([piece.shape[0] for piece in pieces]), pieces[0].shape[1]), BF16),
        compiler_params=params(4),
        cost_estimate=cost(1),
        name=name,
    )(*pieces, *after)


def project_kernel(place, times, gate_ref, weight_ref, *refs):
    parts, shares = refs[:7], refs[7:13]
    total, tail_ref, gates_ref, rows_all, w_all, sems = refs[13:]
    width = total.shape[1]
    group = w_all.shape[0] // 4
    share = group // 8
    mine = place[2]
    own_start = pl.multiple_of(place[1] * width, width)
    own_copy = pltpu.make_async_copy(
        weight_ref.at[:, pl.ds(own_start, width)], w_all.at[pl.ds(0, group), :], sems.at[0]
    )
    own_copy.start()
    used = 0
    for part in parts:
        rows_all[:, used : used + part.shape[1]] = part[...]
        used += part.shape[1]
    gates_ref[...] = jnp.zeros(gates_ref.shape, BF16)
    for video in range(times.shape[0]):
        for index, piece in enumerate(three_pieces(gate_ref[pl.ds(times[video], 1), :])):
            gates_ref[index * 16 + video : index * 16 + video + 1, :] = piece.astype(BF16)
    for core in range(2):
        near, far, other = shares[3 * core : 3 * core + 3]
        pieces = [(near, 0, 0, 0), (far, 0, 0, 4)]
        for step in (1, 2):
            pieces += [
                (near, (step + 1) * share, step, 0),
                (far, (step + 1) * share, step, 4),
                (other, (step - 1) * share, step, 1),
                (other, (step + 1) * share, step, 5),
            ]
        for ref, low, step, flip in pieces:
            count = share if step else 2 * share
            index = mine ^ (flip + 2 * core) if step else place[3] ^ (flip // 2 + core)
            start = pl.multiple_of((1 + step) * group + index * count, share)
            w_all[pl.ds(start, count), :] = ref[low : low + count, :]
    tail_ref[...] = w_all[used:, :]
    own_copy.wait()
    for low in range(0, width, 256):
        block = slice(low, low + 256)
        total[:, block] = jnp.dot(rows_all[...], w_all[0:used, block], preferred_element_type=F32)


def finish_kernel(place, near_ref, far_ref, total, tail_ref, gates_ref, late_ref, out_hbm, out_ref, sems):
    rows, width = out_ref.shape
    half = rows // 2
    me = place[0]
    videos = lax.rem(lax.broadcasted_iota(jnp.int32, (rows, gates_ref.shape[0]), 1), 16).astype(F32)
    marks = jnp.concatenate([near_ref[2:3, :half], far_ref[2:3, half:]], axis=1)
    picked = (column(marks) == 4.0 * videos).astype(BF16)
    copies = []
    for low in range(0, width, 256):
        block = slice(low, low + 256)
        gates = jnp.dot(picked, gates_ref[:, block], preferred_element_type=F32)
        mixed = total[:, block] + jnp.dot(late_ref[...], tail_ref[:, block], preferred_element_type=F32)
        out_ref[:, block] = (mixed * gates).astype(BF16)
        for part in range(2):
            start = me * half if part == 0 else (1 - me) * half
            copies.append(
                pltpu.make_async_copy(
                    out_ref.at[pl.ds(part * half, half), block],
                    out_hbm.at[pl.ds(pl.multiple_of(start, half), half), block],
                    sems.at[len(copies)],
                )
            )
            copies[-1].start()
    for copy in copies:
        copy.wait()


def fast_local(
    query_raw, key_raw, value_rows, query_gain, key_gain, segment, destination, timestep, out_weight, gate_table
):
    rows, width = query_raw.shape
    half = rows // 2
    out_width = gate_table.shape[1]
    total_width = width * lax.axis_size("head")
    ctx, head, batch = lax.axis_index("ctx"), lax.axis_index("head"), lax.axis_index("batch")
    mine = batch * 2 + ctx
    place = jnp.stack([ctx, head, mine, batch]).astype(jnp.int32)
    cuts, low = [], 0
    for count in SENDS:
        cuts.append((low * HD, (low + count) * HD))
        low += count
    assert low * HD == width
    share = width // 8
    packed_shapes = [jax.ShapeDtypeStruct((half + 2 * rows, high - low), BF16) for low, high in cuts]
    in_hbm = functools.partial(pltpu.with_memory_space_constraint, memory_space=pltpu.HBM)
    weight_hbm = in_hbm(out_weight)

    own_queries, other_queries, packed, stats, keys, values, *cut_weights = pl.pallas_call(
        functools.partial(prepare_kernel, cuts[0]),
        in_specs=[SMEM] + [HBM] * 6,
        out_specs=[VMEM] * 9,
        out_shape=[
            jax.ShapeDtypeStruct((half, width), BF16),
            jax.ShapeDtypeStruct((half, width), BF16),
            packed_shapes[0],
            jax.ShapeDtypeStruct((8, rows), F32),
            jax.ShapeDtypeStruct((rows, width), BF16),
            jax.ShapeDtypeStruct((rows, width), BF16),
            jax.ShapeDtypeStruct((2 * share, out_width), BF16),
            jax.ShapeDtypeStruct((share, out_width), BF16),
            jax.ShapeDtypeStruct((share, out_width), BF16),
        ],
        scratch_shapes=[
            pltpu.VMEM((rows, width), BF16),
            pltpu.VMEM((1, rows), jnp.int32),
            pltpu.VMEM((1, rows), jnp.int32),
            pltpu.SemaphoreType.DMA((8,)),
        ],
        compiler_params=params(16),
        cost_estimate=cost(2),
        name="prepare",
    )(
        place, in_hbm(query_raw), in_hbm(key_raw), in_hbm(value_rows),
        in_hbm(destination.reshape(1, rows)), in_hbm(segment.reshape(1, rows)), weight_hbm,
    )
    from_head = [lax.ppermute(cut_weights[s - 1], "head", xor_pairs(4, s)) for s in (1, 2, 3)]
    arrived = [lax.ppermute(packed, "ctx", SWAP_CTX)]
    near = pl.pallas_call(
        settle_kernel,
        in_specs=[VMEM] * 4,
        out_specs=VMEM,
        out_shape=jax.ShapeDtypeStruct((8, rows), F32),
        compiler_params=params(4),
        cost_estimate=cost(1),
        name="settle",
    )(stats, *[lax.ppermute(stats, "head", xor_pairs(4, step)) for step in (1, 2, 3)])
    far = lax.ppermute(near, "ctx", SWAP_CTX)

    def attend(cut, piece, after):
        return pl.pallas_call(
            functools.partial(attend_kernel, cut, total_width),
            in_specs=[VMEM] * 8 + [AFTER] * len(after),
            out_specs=VMEM,
            out_shape=jax.ShapeDtypeStruct((rows, cut[1] - cut[0]), BF16),
            compiler_params=params(14),
            cost_estimate=cost(8),
            name="attend",
        )(
            near, far, own_queries, keys, values, query_gain.reshape(1, width),
            key_gain.reshape(1, width), piece, *after,
        )

    def spread(attended):
        one = lax.ppermute(attended, "head", xor_pairs(4, 1))
        two = lax.ppermute(attended, "head", xor_pairs(4, 2))
        three = lax.ppermute(two, "head", xor_pairs(4, 1))
        return [attended, one, two, three]

    first = spread(attend(cuts[0], arrived[0], [gate([far, arrived[0]], 10, "ready")]))
    clear = gate([from_head[1], first[0]], 10, "clear")
    packed = pl.pallas_call(
        functools.partial(pack_kernel, cuts[1]),
        in_specs=[VMEM] * 3 + [AFTER],
        out_specs=VMEM,
        out_shape=packed_shapes[1],
        compiler_params=params(4),
        cost_estimate=cost(1),
        name="pack",
    )(other_queries, keys, values, clear)
    arrived.append(lax.ppermute(packed, "ctx", SWAP_CTX))
    landed = gate([*from_head, packed], 10, "landed")
    two_three = join(from_head[1:], [packed], "join_two")
    share0 = join(from_head, [packed], "join_all")
    share_y = lax.ppermute(two_three, "ctx", SWAP_CTX)
    share_x = lax.ppermute(share0, "batch", SWAP_X)

    token = gate(first[1:3], 10, "token")
    attended = attend(cuts[1], arrived[1], [token])
    share_y = join([share_y], [attended, share_x], "hold")
    share_xy = lax.ppermute(share_y, "batch", SWAP_X)
    last = spread(attended)
    passed = gate([first[3], *last[1:3]], 10, "passed")
    share_yxy = join([share_y, share_xy], [passed], "join_y")
    shares = [share0, share_x, share_yxy]
    shares += [lax.ppermute(value, "batch", SWAP_CORE) for value in shares]

    parts = [first[0], last[0], first[1], last[1], first[2], last[2], first[3]]
    used = 3 * width + cuts[0][1]
    total, tail_weights, gates = pl.pallas_call(
        project_kernel,
        in_specs=[SMEM, SMEM, VMEM, HBM] + [VMEM] * (len(parts) + len(shares)),
        out_specs=[VMEM] * 3,
        out_shape=[
            jax.ShapeDtypeStruct((rows, out_width), F32),
            jax.ShapeDtypeStruct((4 * width - used, out_width), BF16),
            jax.ShapeDtypeStruct((48, out_width), BF16),
        ],
        scratch_shapes=[
            pltpu.VMEM((rows, used), BF16),
            pltpu.VMEM((4 * width, out_width), BF16),
            pltpu.SemaphoreType.DMA((1,)),
        ],
        compiler_params=params(24),
        cost_estimate=cost(0),
        name="project",
    )(place, timestep, gate_table, weight_hbm, *parts, *shares)
    return pl.pallas_call(
        finish_kernel,
        in_specs=[SMEM] + [VMEM] * 6,
        out_specs=ANY,
        out_shape=jax.ShapeDtypeStruct((rows, out_width), BF16),
        scratch_shapes=[
            pltpu.VMEM((rows, out_width), BF16),
            pltpu.SemaphoreType.DMA((2 * out_width // 256,)),
        ],
        compiler_params=params(14),
        cost_estimate=cost(0),
        name="finish",
    )(place, near, far, total, tail_weights, gates, last[3])


def for_sending(array):

    def short(part):
        return part.astype(jnp.bfloat16) if part.dtype == jnp.float32 else part

    return jax.tree.map(short, array)


def attend(running, queries, query_mark, key_rows, value_part, key_mark, head_count, score_scale):
    maxima, totals, accumulated = running
    query_count = queries.shape[0]
    query_heads = queries.reshape(query_count, head_count, HD)
    key_heads = key_rows.reshape(key_rows.shape[0], head_count, HD)
    value_heads = value_part.reshape(value_part.shape[0], head_count, HD)
    scores = (
        jnp.einsum("qhd,khd->hqk", query_heads, key_heads, preferred_element_type=jnp.float32)
        * score_scale
    )
    allowed = (query_mark[:, None] == key_mark[None, :])[None]
    scores = jnp.where(allowed, scores, -1e30)
    new_max = jnp.maximum(maxima, jnp.max(scores, axis=2))
    factor = jnp.exp(maxima - new_max)
    weights = jnp.where(allowed, jnp.exp(scores - new_max[:, :, None]), 0.0)
    totals = totals * factor + jnp.sum(weights, axis=2)
    update = jnp.einsum(
        "hqk,khd->qhd",
        weights.astype(jnp.bfloat16),
        value_heads,
        preferred_element_type=jnp.float32,
    )
    accumulated = accumulated * jnp.transpose(factor)[:, :, None] + update
    return (new_max, totals, accumulated)


def attend_blocks(
    running, queries, query_mark, key_rows, value_part, key_mark, head_count, score_scale
):
    block_rows = queries.shape[0]
    block_count = key_rows.shape[0] // block_rows
    stacked = (
        key_rows.reshape(block_count, block_rows, key_rows.shape[1]),
        value_part.reshape(block_count, block_rows, value_part.shape[1]),
        key_mark.reshape(block_count, block_rows),
    )

    def advance(state, shard_piece):
        return (
            attend(
                state,
                queries,
                query_mark,
                shard_piece[0],
                shard_piece[1],
                shard_piece[2],
                head_count,
                score_scale,
            ),
            None,
        )

    running, unused = lax.scan(advance, running, stacked)
    return running


def general_local(
    query_raw,
    key_raw,
    value_rows,
    query_gain,
    key_gain,
    segment,
    destination,
    timestep,
    out_weight,
    gate_table,
):
    row_count = query_raw.shape[0]
    row_width = query_raw.shape[1]
    head_count = row_width // HD
    ctx_size = lax.axis_size("ctx")
    total_width = row_width * lax.axis_size("head")
    score_scale = 1.0 / math.sqrt(HD)
    query_float = query_raw.astype(jnp.float32)
    key_float = key_raw.astype(jnp.float32)
    query_sum, key_sum = lax.psum(
        (jnp.sum(query_float * query_float, axis=1), jnp.sum(key_float * key_float, axis=1)), "head"
    )
    queries = (
        query_float * lax.rsqrt(query_sum / total_width + 1e-06)[:, None] * query_gain
    ).astype(jnp.bfloat16)
    normed_keys = (key_float * lax.rsqrt(key_sum / total_width + 1e-06)[:, None] * key_gain).astype(
        jnp.bfloat16
    )
    slot_count = row_count // ctx_size
    target = destination // row_count * slot_count + destination % slot_count

    def placed(array):
        return jnp.zeros_like(array).at[target].set(array)

    initial = (
        jnp.full((head_count, row_count), -1e30, jnp.float32),
        jnp.zeros((head_count, row_count), jnp.float32),
        jnp.zeros((row_count, head_count, HD), jnp.float32),
    )
    own_queries, own_keys, own_values, own_segment = (
        lax.all_to_all(placed(queries), "ctx", split_axis=0, concat_axis=0, tiled=True),
        lax.all_to_all(placed(normed_keys), "ctx", split_axis=0, concat_axis=0, tiled=True),
        lax.all_to_all(placed(value_rows), "ctx", split_axis=0, concat_axis=0, tiled=True),
        lax.all_to_all(placed(segment), "ctx", split_axis=0, concat_axis=0, tiled=True),
    )
    running = attend_blocks(
        initial,
        own_queries,
        own_segment,
        lax.all_gather(own_keys, "ctx", axis=0, tiled=True),
        lax.all_gather(own_values, "ctx", axis=0, tiled=True),
        lax.all_gather(for_sending(own_segment), "ctx", axis=0, tiled=True),
        head_count,
        score_scale,
    )
    attended = (
        (running[2] / jnp.transpose(running[1])[:, :, None])
        .reshape(row_count, row_width)
        .astype(jnp.bfloat16)
    )
    head_terms = jnp.dot(attended, out_weight, preferred_element_type=jnp.float32)
    mixed_rows = lax.psum_scatter(
        head_terms.astype(jnp.bfloat16), "head", scatter_dimension=1, tiled=True
    ).astype(jnp.float32)
    video_gates = jnp.dot(
        jax.nn.one_hot(timestep, gate_table.shape[0], dtype=jnp.float32),
        gate_table,
        precision=lax.Precision.HIGHEST,
    )
    token_gates = jnp.dot(
        jax.nn.one_hot(own_segment, timestep.shape[0], dtype=jnp.float32),
        video_gates,
        precision=lax.Precision.HIGHEST,
    )
    return (mixed_rows * token_gates).astype(jnp.bfloat16)


def solution(mesh):
    placed = (
        P(("batch", "ctx"), "head"),
        P(("batch", "ctx"), "head"),
        P(("batch", "ctx"), "head"),
        P("head"),
        P("head"),
        P(("batch", "ctx")),
        P(("batch", "ctx")),
        P("batch"),
        P("head", None),
        P(None, "head"),
    )
    sizes = dict(mesh.shape)
    fast = sizes["batch"] == 4 and sizes["ctx"] == 2 and sizes["head"] == 4
    local = fast_local if fast else general_local
    return jax.shard_map(
        local, mesh=mesh, in_specs=placed, out_specs=P(("batch", "ctx"), "head"), check_vma=False
    )
```

```python
import functools
import math

import jax
import jax.numpy as jnp
from jax import lax
from jax.experimental import pallas as pl
from jax.experimental.pallas import tpu as pltpu
from jax.sharding import PartitionSpec as P

HD = 128
F32 = jnp.float32
BF16 = jnp.bfloat16
VMEM = pl.BlockSpec(memory_space=pltpu.VMEM)
SMEM = pl.BlockSpec(memory_space=pltpu.SMEM)
ANY = pl.BlockSpec(memory_space=pl.ANY)
HBM = pl.BlockSpec(memory_space=pltpu.HBM)
AFTER = VMEM
SENDS = (3, 2)

SWAP_CTX = ((0, 1), (1, 0))
SWAP_CORE = ((0, 1), (1, 0), (2, 3), (3, 2))
SWAP_X = ((0, 2), (2, 0), (1, 3), (3, 1))


def xor_pairs(size, step):
    return tuple((i, i ^ step) for i in range(size))


def params(mebibytes):
    return pltpu.CompilerParams(vmem_limit_bytes=mebibytes * 1024 * 1024)


def cost(microseconds):
    return pl.CostEstimate(flops=0, bytes_accessed=int(microseconds * 3_600_000), transcendentals=0)


def load(pairs, sems):
    copies = [pltpu.make_async_copy(source, target, sems.at[i]) for i, (source, target) in enumerate(pairs)]
    for copy in copies:
        copy.start()
    return copies


def row_sums(values):
    squares = values * values
    folded = squares[:, 0:HD]
    for low in range(HD, values.shape[1], HD):
        folded = folded + squares[:, low : low + HD]
    return jnp.sum(jnp.transpose(folded), axis=0, keepdims=True)


def three_pieces(value):
    pieces = []
    for _ in range(3):
        short = value.astype(BF16).astype(F32)
        pieces.append(short)
        value = value - short
    return pieces


def column(row):
    return jnp.transpose(jnp.broadcast_to(row, (8, row.shape[1])))[:, 0:1]


def prepare_kernel(
    cut, place, q_hbm, k_hbm, v_hbm, dest_hbm, seg_hbm, weight_ref,
    own_ref, other_ref, packed_ref, stats_ref, k_ref, v_ref, one_ref, two_ref, three_ref,
    q_ref, dest_ref, seg_ref, sems,
):
    pairs = [(dest_hbm, dest_ref), (seg_hbm, seg_ref), (q_hbm, q_ref), (k_hbm, k_ref), (v_hbm, v_ref)]
    for step, (ref, index) in enumerate(((one_ref, place[3]), (two_ref, place[2]), (three_ref, place[2]))):
        count, columns = ref.shape
        first = pl.multiple_of(index * count, count)
        start = pl.multiple_of((place[1] ^ (step + 1)) * columns, columns)
        pairs.append((weight_ref.at[pl.ds(first, count), pl.ds(start, columns)], ref))
    copies = load(pairs, sems)
    rows = q_ref.shape[0]
    half = rows // 2
    low, high = cut
    me = place[0]
    copies[0].wait()
    copies[1].wait()
    dest = dest_ref[...]
    block = (dest >= rows).astype(jnp.int32)
    slot = dest - block * rows - me * half + jnp.where(block == me, 0, half)
    spread = (lax.broadcasted_iota(jnp.int32, (rows, rows), 0) == slot).astype(BF16)
    marks = seg_ref[...].astype(F32)
    moved_marks = lax.dot_general(
        jnp.broadcast_to(marks, (8, rows)).astype(BF16), spread, (((1,), (1,)), ((), ())),
        preferred_element_type=F32,
    )[0:1]
    copies[2].wait()
    moved = jnp.dot(spread, q_ref[...], preferred_element_type=F32)
    moved_short = moved.astype(BF16)
    own_ref[...] = moved_short[:half]
    other_ref[...] = moved_short[half:]
    packed_ref[0:half, :] = moved_short[half:, low:high]
    query_sums = row_sums(moved)
    copies[3].wait()
    packed_ref[half : half + rows, :] = k_ref[:, low:high]
    key_sums = row_sums(k_ref[...].astype(F32))
    stats_ref[...] = jnp.concatenate(
        [query_sums, key_sums, moved_marks, marks, jnp.full((4, rows), me).astype(F32)], axis=0
    )
    copies[4].wait()
    packed_ref[half + rows :, :] = v_ref[:, low:high]
    for copy in copies[5:]:
        copy.wait()


def settle_kernel(own_ref, one_ref, two_ref, three_ref, out_ref):
    out_ref[...] = (own_ref[...] + one_ref[...]) + (two_ref[...] + three_ref[...])


def pack_kernel(cut, other_ref, k_ref, v_ref, *refs):
    out_ref = refs[-1]
    low, high = cut
    half, rows = other_ref.shape[0], k_ref.shape[0]
    out_ref[0:half, :] = other_ref[:, low:high]
    out_ref[half : half + rows, :] = k_ref[:, low:high]
    out_ref[half + rows :, :] = v_ref[:, low:high]


def attend_kernel(
    cut, total_width, near_ref, far_ref, q_ref, k_ref, v_ref, qg_ref, kg_ref, remote_ref, *refs
):
    out_ref = refs[-1]
    rows = k_ref.shape[0]
    half = rows // 2
    near, far = near_ref[...], far_ref[...]
    near_factors = lax.rsqrt(near[0:2] / total_width + 1e-06)
    far_factors = lax.rsqrt(far[0:2] / total_width + 1e-06)
    q_mark = jnp.concatenate([near[2:3, :half], far[2:3, half:]], axis=1)
    k_mark = jnp.concatenate([near[3:4], far[3:4]], axis=1)
    q_factor = column(jnp.concatenate([near_factors[0:1, :half], far_factors[0:1, half:]], axis=1))
    k_factor = column(jnp.concatenate([near_factors[1:2], far_factors[1:2]], axis=1))
    lane_video = 4.0 * lax.broadcasted_iota(jnp.int32, (2 * rows, HD), 1).astype(F32)
    q_video = jnp.where(column(q_mark) == lane_video[:rows], 1.0, 0.0).astype(BF16)
    k_video = jnp.where(column(k_mark) == lane_video, 0.0, -(2.0**20)).astype(BF16)
    ones = jnp.ones((2 * rows, HD), BF16)
    scale = math.log2(math.e) / math.sqrt(HD)
    first, last = cut
    for low in range(first, last, HD):
        here = slice(low - first, low - first + HD)
        wide = slice(low, low + HD)
        queries = jnp.concatenate([q_ref[:, wide], remote_ref[0:half, here]], axis=0)
        keys = jnp.concatenate([k_ref[:, wide], remote_ref[half : half + rows, here]], axis=0)
        values = jnp.concatenate([v_ref[:, wide], remote_ref[half + rows :, here]], axis=0)
        queries = (queries.astype(F32) * q_factor * qg_ref[0:1, wide]).astype(BF16)
        keys = (keys.astype(F32) * k_factor * kg_ref[0:1, wide]).astype(BF16)
        queries = jnp.concatenate([queries, q_video], axis=1)
        keys = jnp.concatenate([keys, k_video], axis=1)
        values = jnp.concatenate([values, ones], axis=1)
        for part in range(2):
            piece = slice(part * half, (part + 1) * half)
            scores = lax.dot_general(
                queries[piece], keys, (((1,), (1,)), ((), ())), preferred_element_type=F32
            )
            largest = jnp.max(scores, axis=1, keepdims=True)
            weights = jnp.exp2((scores - largest) * scale).astype(BF16)
            mixed = jnp.dot(weights, values, preferred_element_type=F32)
            mixed, totals = mixed[:, :HD], mixed[:, HD:]
            out_ref[piece, here] = (mixed / totals).astype(BF16)


def join_kernel(count, *refs):
    low = 0
    for ref in refs[:count]:
        refs[-1][low : low + ref.shape[0], :] = ref[...]
        low += ref.shape[0]


def gate_kernel(*refs):
    refs[-1][...] = jnp.zeros(refs[-1].shape, F32)


def gate(after, weight, name):
    return pl.pallas_call(
        gate_kernel,
        in_specs=[AFTER] * len(after),
        out_specs=VMEM,
        out_shape=jax.ShapeDtypeStruct((8, 128), F32),
        compiler_params=params(4),
        cost_estimate=pl.CostEstimate(flops=weight * 900_000_000, bytes_accessed=4096, transcendentals=0),
        name=name,
    )(*after)


def join(pieces, after, name):
    return pl.pallas_call(
        functools.partial(join_kernel, len(pieces)),
        in_specs=[VMEM] * len(pieces) + [AFTER] * len(after),
        out_specs=VMEM,
        out_shape=jax.ShapeDtypeStruct((sum([piece.shape[0] for piece in pieces]), pieces[0].shape[1]), BF16),
        compiler_params=params(4),
        cost_estimate=cost(1),
        name=name,
    )(*pieces, *after)


def project_kernel(place, times, gate_ref, weight_ref, *refs):
    parts, shares = refs[:7], refs[7:13]
    total, tail_ref, gates_ref, rows_all, w_all, sems = refs[13:]
    width = total.shape[1]
    group = w_all.shape[0] // 4
    share = group // 8
    mine = place[2]
    own_start = pl.multiple_of(place[1] * width, width)
    own_copy = pltpu.make_async_copy(
        weight_ref.at[:, pl.ds(own_start, width)], w_all.at[pl.ds(0, group), :], sems.at[0]
    )
    own_copy.start()
    used = 0
    for part in parts:
        rows_all[:, used : used + part.shape[1]] = part[...]
        used += part.shape[1]
    chosen = [gate_ref[pl.ds(times[video], 1), :] for video in range(times.shape[0])]
    chosen.append(jnp.zeros((16 - len(chosen), width), F32))
    chosen = jnp.concatenate(chosen, axis=0)
    gates_ref[...] = jnp.concatenate(three_pieces(chosen), axis=0).astype(BF16)
    for core in range(2):
        near, far, other = shares[3 * core : 3 * core + 3]
        pieces = [(near, 0, 0, 0), (far, 0, 0, 4)]
        for step in (1, 2):
            pieces += [
                (near, (step + 1) * share, step, 0),
                (far, (step + 1) * share, step, 4),
                (other, (step - 1) * share, step, 1),
                (other, (step + 1) * share, step, 5),
            ]
        for ref, low, step, flip in pieces:
            count = share if step else 2 * share
            index = mine ^ (flip + 2 * core) if step else place[3] ^ (flip // 2 + core)
            start = pl.multiple_of((1 + step) * group + index * count, share)
            w_all[pl.ds(start, count), :] = ref[low : low + count, :]
    tail_ref[...] = w_all[used:, :]
    own_copy.wait()
    for low in range(0, width, 256):
        block = slice(low, low + 256)
        total[:, block] = jnp.dot(rows_all[...], w_all[0:used, block], preferred_element_type=F32)


def finish_kernel(near_ref, far_ref, total, tail_ref, gates_ref, late_ref, out_hbm, out_ref, sems):
    rows, width = out_ref.shape
    half = rows // 2
    second = near_ref[4:5, 0:1] > 0.5
    videos = lax.rem(lax.broadcasted_iota(jnp.int32, (rows, gates_ref.shape[0]), 1), 16).astype(F32)
    marks = jnp.concatenate([near_ref[2:3, :half], far_ref[2:3, half:]], axis=1)
    picked = (column(marks) == 4.0 * videos).astype(BF16)
    copies = []
    for low in range(0, width, 256):
        block = slice(low, low + 256)
        gates = jnp.dot(picked, gates_ref[:, block], preferred_element_type=F32)
        mixed = total[:, block] + jnp.dot(late_ref[...], tail_ref[:, block], preferred_element_type=F32)
        gated = mixed * gates
        out_ref[0:half, block] = jnp.where(second, gated[half:], gated[:half]).astype(BF16)
        out_ref[half:, block] = jnp.where(second, gated[:half], gated[half:]).astype(BF16)
        copies.append(pltpu.make_async_copy(out_ref.at[:, block], out_hbm.at[:, block], sems.at[len(copies)]))
        copies[-1].start()
    for copy in copies:
        copy.wait()


def fast_local(
    query_raw, key_raw, value_rows, query_gain, key_gain, segment, destination, timestep, out_weight, gate_table
):
    rows, width = query_raw.shape
    half = rows // 2
    out_width = gate_table.shape[1]
    total_width = width * lax.axis_size("head")
    ctx, head, batch = lax.axis_index("ctx"), lax.axis_index("head"), lax.axis_index("batch")
    mine = batch * 2 + ctx
    place = jnp.stack([ctx, head, mine, batch]).astype(jnp.int32)
    cuts, low = [], 0
    for count in SENDS:
        cuts.append((low * HD, (low + count) * HD))
        low += count
    assert low * HD == width
    share = width // 8
    packed_shapes = [jax.ShapeDtypeStruct((half + 2 * rows, high - low), BF16) for low, high in cuts]
    in_hbm = functools.partial(pltpu.with_memory_space_constraint, memory_space=pltpu.HBM)
    weight_hbm = in_hbm(out_weight)

    own_queries, other_queries, packed, stats, keys, values, *cut_weights = pl.pallas_call(
        functools.partial(prepare_kernel, cuts[0]),
        in_specs=[SMEM] + [HBM] * 6,
        out_specs=[VMEM] * 9,
        out_shape=[
            jax.ShapeDtypeStruct((half, width), BF16),
            jax.ShapeDtypeStruct((half, width), BF16),
            packed_shapes[0],
            jax.ShapeDtypeStruct((8, rows), F32),
            jax.ShapeDtypeStruct((rows, width), BF16),
            jax.ShapeDtypeStruct((rows, width), BF16),
            jax.ShapeDtypeStruct((2 * share, out_width), BF16),
            jax.ShapeDtypeStruct((share, out_width), BF16),
            jax.ShapeDtypeStruct((share, out_width), BF16),
        ],
        scratch_shapes=[
            pltpu.VMEM((rows, width), BF16),
            pltpu.VMEM((1, rows), jnp.int32),
            pltpu.VMEM((1, rows), jnp.int32),
            pltpu.SemaphoreType.DMA((8,)),
        ],
        compiler_params=params(16),
        cost_estimate=cost(2),
        name="prepare",
    )(
        place, in_hbm(query_raw), in_hbm(key_raw), in_hbm(value_rows),
        in_hbm(destination.reshape(1, rows)), in_hbm(segment.reshape(1, rows)), weight_hbm,
    )
    from_head = [lax.ppermute(cut_weights[s - 1], "head", xor_pairs(4, s)) for s in (1, 2, 3)]
    arrived = [lax.ppermute(packed, "ctx", SWAP_CTX)]
    near = pl.pallas_call(
        settle_kernel,
        in_specs=[VMEM] * 4,
        out_specs=VMEM,
        out_shape=jax.ShapeDtypeStruct((8, rows), F32),
        compiler_params=params(4),
        cost_estimate=cost(1),
        name="settle",
    )(stats, *[lax.ppermute(stats, "head", xor_pairs(4, step)) for step in (1, 2, 3)])
    far = lax.ppermute(near, "ctx", SWAP_CTX)

    def attend(cut, piece, after):
        return pl.pallas_call(
            functools.partial(attend_kernel, cut, total_width),
            in_specs=[VMEM] * 8 + [AFTER] * len(after),
            out_specs=VMEM,
            out_shape=jax.ShapeDtypeStruct((rows, cut[1] - cut[0]), BF16),
            compiler_params=params(14),
            cost_estimate=cost(8),
            name="attend",
        )(
            near, far, own_queries, keys, values, query_gain.reshape(1, width),
            key_gain.reshape(1, width), piece, *after,
        )

    def spread(attended):
        one = lax.ppermute(attended, "head", xor_pairs(4, 1))
        two = lax.ppermute(attended, "head", xor_pairs(4, 2))
        three = lax.ppermute(two, "head", xor_pairs(4, 1))
        return [attended, one, two, three]

    first = spread(attend(cuts[0], arrived[0], [gate([far, arrived[0]], 10, "ready")]))
    clear = gate([from_head[1], first[0]], 10, "clear")
    packed = pl.pallas_call(
        functools.partial(pack_kernel, cuts[1]),
        in_specs=[VMEM] * 3 + [AFTER],
        out_specs=VMEM,
        out_shape=packed_shapes[1],
        compiler_params=params(4),
        cost_estimate=cost(1),
        name="pack",
    )(other_queries, keys, values, clear)
    arrived.append(lax.ppermute(packed, "ctx", SWAP_CTX))
    landed = gate([*from_head, packed], 10, "landed")
    two_three = join(from_head[1:], [packed], "join_two")
    share0 = join(from_head, [packed], "join_all")
    share_y = lax.ppermute(two_three, "ctx", SWAP_CTX)
    share_x = lax.ppermute(share0, "batch", SWAP_X)

    token = gate(first[1:3], 10, "token")
    attended = attend(cuts[1], arrived[1], [token])
    share_y = join([share_y], [attended, share_x], "hold")
    share_xy = lax.ppermute(share_y, "batch", SWAP_X)
    last = spread(attended)
    passed = gate([first[3], *last[1:3]], 10, "passed")
    share_yxy = join([share_y, share_xy], [passed], "join_y")
    shares = [share0, share_x, share_yxy]
    shares += [lax.ppermute(value, "batch", SWAP_CORE) for value in shares]

    parts = [first[0], last[0], first[1], last[1], first[2], last[2], first[3]]
    used = 3 * width + cuts[0][1]
    total, tail_weights, gates = pl.pallas_call(
        project_kernel,
        in_specs=[SMEM, SMEM, VMEM, HBM] + [VMEM] * (len(parts) + len(shares)),
        out_specs=[VMEM] * 3,
        out_shape=[
            jax.ShapeDtypeStruct((rows, out_width), F32),
            jax.ShapeDtypeStruct((4 * width - used, out_width), BF16),
            jax.ShapeDtypeStruct((48, out_width), BF16),
        ],
        scratch_shapes=[
            pltpu.VMEM((rows, used), BF16),
            pltpu.VMEM((4 * width, out_width), BF16),
            pltpu.SemaphoreType.DMA((1,)),
        ],
        compiler_params=params(24),
        cost_estimate=cost(0),
        name="project",
    )(place, timestep, gate_table, weight_hbm, *parts, *shares)
    return pl.pallas_call(
        finish_kernel,
        in_specs=[VMEM] * 6,
        out_specs=ANY,
        out_shape=jax.ShapeDtypeStruct((rows, out_width), BF16),
        scratch_shapes=[
            pltpu.VMEM((rows, out_width), BF16),
            pltpu.SemaphoreType.DMA((out_width // 256,)),
        ],
        compiler_params=params(14),
        cost_estimate=cost(0),
        name="finish",
    )(near, far, total, tail_weights, gates, last[3])


def for_sending(array):

    def short(part):
        return part.astype(jnp.bfloat16) if part.dtype == jnp.float32 else part

    return jax.tree.map(short, array)


def attend(running, queries, query_mark, key_rows, value_part, key_mark, head_count, score_scale):
    maxima, totals, accumulated = running
    query_count = queries.shape[0]
    query_heads = queries.reshape(query_count, head_count, HD)
    key_heads = key_rows.reshape(key_rows.shape[0], head_count, HD)
    value_heads = value_part.reshape(value_part.shape[0], head_count, HD)
    scores = (
        jnp.einsum("qhd,khd->hqk", query_heads, key_heads, preferred_element_type=jnp.float32)
        * score_scale
    )
    allowed = (query_mark[:, None] == key_mark[None, :])[None]
    scores = jnp.where(allowed, scores, -1e30)
    new_max = jnp.maximum(maxima, jnp.max(scores, axis=2))
    factor = jnp.exp(maxima - new_max)
    weights = jnp.where(allowed, jnp.exp(scores - new_max[:, :, None]), 0.0)
    totals = totals * factor + jnp.sum(weights, axis=2)
    update = jnp.einsum(
        "hqk,khd->qhd",
        weights.astype(jnp.bfloat16),
        value_heads,
        preferred_element_type=jnp.float32,
    )
    accumulated = accumulated * jnp.transpose(factor)[:, :, None] + update
    return (new_max, totals, accumulated)


def attend_blocks(
    running, queries, query_mark, key_rows, value_part, key_mark, head_count, score_scale
):
    block_rows = queries.shape[0]
    block_count = key_rows.shape[0] // block_rows
    stacked = (
        key_rows.reshape(block_count, block_rows, key_rows.shape[1]),
        value_part.reshape(block_count, block_rows, value_part.shape[1]),
        key_mark.reshape(block_count, block_rows),
    )

    def advance(state, shard_piece):
        return (
            attend(
                state,
                queries,
                query_mark,
                shard_piece[0],
                shard_piece[1],
                shard_piece[2],
                head_count,
                score_scale,
            ),
            None,
        )

    running, unused = lax.scan(advance, running, stacked)
    return running


def general_local(
    query_raw,
    key_raw,
    value_rows,
    query_gain,
    key_gain,
    segment,
    destination,
    timestep,
    out_weight,
    gate_table,
):
    row_count = query_raw.shape[0]
    row_width = query_raw.shape[1]
    head_count = row_width // HD
    ctx_size = lax.axis_size("ctx")
    total_width = row_width * lax.axis_size("head")
    score_scale = 1.0 / math.sqrt(HD)
    query_float = query_raw.astype(jnp.float32)
    key_float = key_raw.astype(jnp.float32)
    query_sum, key_sum = lax.psum(
        (jnp.sum(query_float * query_float, axis=1), jnp.sum(key_float * key_float, axis=1)), "head"
    )
    queries = (
        query_float * lax.rsqrt(query_sum / total_width + 1e-06)[:, None] * query_gain
    ).astype(jnp.bfloat16)
    normed_keys = (key_float * lax.rsqrt(key_sum / total_width + 1e-06)[:, None] * key_gain).astype(
        jnp.bfloat16
    )
    slot_count = row_count // ctx_size
    target = destination // row_count * slot_count + destination % slot_count

    def placed(array):
        return jnp.zeros_like(array).at[target].set(array)

    initial = (
        jnp.full((head_count, row_count), -1e30, jnp.float32),
        jnp.zeros((head_count, row_count), jnp.float32),
        jnp.zeros((row_count, head_count, HD), jnp.float32),
    )
    own_queries, own_keys, own_values, own_segment = (
        lax.all_to_all(placed(queries), "ctx", split_axis=0, concat_axis=0, tiled=True),
        lax.all_to_all(placed(normed_keys), "ctx", split_axis=0, concat_axis=0, tiled=True),
        lax.all_to_all(placed(value_rows), "ctx", split_axis=0, concat_axis=0, tiled=True),
        lax.all_to_all(placed(segment), "ctx", split_axis=0, concat_axis=0, tiled=True),
    )
    running = attend_blocks(
        initial,
        own_queries,
        own_segment,
        lax.all_gather(own_keys, "ctx", axis=0, tiled=True),
        lax.all_gather(own_values, "ctx", axis=0, tiled=True),
        lax.all_gather(for_sending(own_segment), "ctx", axis=0, tiled=True),
        head_count,
        score_scale,
    )
    attended = (
        (running[2] / jnp.transpose(running[1])[:, :, None])
        .reshape(row_count, row_width)
        .astype(jnp.bfloat16)
    )
    head_terms = jnp.dot(attended, out_weight, preferred_element_type=jnp.float32)
    mixed_rows = lax.psum_scatter(
        head_terms.astype(jnp.bfloat16), "head", scatter_dimension=1, tiled=True
    ).astype(jnp.float32)
    video_gates = jnp.dot(
        jax.nn.one_hot(timestep, gate_table.shape[0], dtype=jnp.float32),
        gate_table,
        precision=lax.Precision.HIGHEST,
    )
    token_gates = jnp.dot(
        jax.nn.one_hot(own_segment, timestep.shape[0], dtype=jnp.float32),
        video_gates,
        precision=lax.Precision.HIGHEST,
    )
    return (mixed_rows * token_gates).astype(jnp.bfloat16)


def solution(mesh):
    placed = (
        P(("batch", "ctx"), "head"),
        P(("batch", "ctx"), "head"),
        P(("batch", "ctx"), "head"),
        P("head"),
        P("head"),
        P(("batch", "ctx")),
        P(("batch", "ctx")),
        P("batch"),
        P("head", None),
        P(None, "head"),
    )
    sizes = dict(mesh.shape)
    fast = sizes["batch"] == 4 and sizes["ctx"] == 2 and sizes["head"] == 4
    local = fast_local if fast else general_local
    return jax.shard_map(
        local, mesh=mesh, in_specs=placed, out_specs=P(("batch", "ctx"), "head"), check_vma=False
    )
```

```python
import functools
import math

import jax
import jax.numpy as jnp
from jax import lax
from jax.experimental import pallas as pl
from jax.experimental.pallas import tpu as pltpu
from jax.sharding import PartitionSpec as P

HD = 128
F32 = jnp.float32
BF16 = jnp.bfloat16
VMEM = pl.BlockSpec(memory_space=pltpu.VMEM)
SMEM = pl.BlockSpec(memory_space=pltpu.SMEM)
ANY = pl.BlockSpec(memory_space=pl.ANY)
HBM = pl.BlockSpec(memory_space=pltpu.HBM)
AFTER = VMEM
SENDS = (3, 2)

SWAP_CTX = ((0, 1), (1, 0))
SWAP_CORE = ((0, 1), (1, 0), (2, 3), (3, 2))
SWAP_X = ((0, 2), (2, 0), (1, 3), (3, 1))


def xor_pairs(size, step):
    return tuple((i, i ^ step) for i in range(size))


def params(mebibytes):
    return pltpu.CompilerParams(vmem_limit_bytes=mebibytes * 1024 * 1024)


def cost(microseconds):
    return pl.CostEstimate(flops=0, bytes_accessed=int(microseconds * 3_600_000), transcendentals=0)


def load(pairs, sems):
    copies = [pltpu.make_async_copy(source, target, sems.at[i]) for i, (source, target) in enumerate(pairs)]
    for copy in copies:
        copy.start()
    return copies


def row_sums(values):
    squares = values * values
    folded = squares[:, 0:HD]
    for low in range(HD, values.shape[1], HD):
        folded = folded + squares[:, low : low + HD]
    return jnp.sum(jnp.transpose(folded), axis=0, keepdims=True)


def three_pieces(value):
    pieces = []
    for _ in range(3):
        short = value.astype(BF16).astype(F32)
        pieces.append(short)
        value = value - short
    return pieces


def column(row):
    return jnp.transpose(jnp.broadcast_to(row, (8, row.shape[1])))[:, 0:1]


def prepare_kernel(
    cut, after_ref, q_hbm, k_hbm, v_hbm, dest_hbm, seg_hbm, weight_ref,
    own_ref, other_ref, packed_ref, stats_ref, k_ref, v_ref, one_ref, two_ref, three_ref,
    q_ref, dest_ref, seg_ref, sems,
):
    me, head, batch = lax.axis_index("ctx"), lax.axis_index("head"), lax.axis_index("batch")
    mine = batch * 2 + me
    pairs = [(dest_hbm, dest_ref), (seg_hbm, seg_ref), (q_hbm, q_ref), (k_hbm, k_ref), (v_hbm, v_ref)]
    for step, (ref, index) in enumerate(((one_ref, batch), (two_ref, mine), (three_ref, mine))):
        count, columns = ref.shape
        first = pl.multiple_of(index * count, count)
        start = pl.multiple_of((head ^ (step + 1)) * columns, columns)
        pairs.append((weight_ref.at[pl.ds(first, count), pl.ds(start, columns)], ref))
    copies = load(pairs, sems)
    rows = q_ref.shape[0]
    half = rows // 2
    low, high = cut
    copies[0].wait()
    copies[1].wait()
    dest = dest_ref[...]
    block = (dest >= rows).astype(jnp.int32)
    slot = dest - block * rows - me * half + jnp.where(block == me, 0, half)
    spread = (lax.broadcasted_iota(jnp.int32, (rows, rows), 0) == slot).astype(BF16)
    marks = seg_ref[...].astype(F32)
    moved_marks = lax.dot_general(
        jnp.broadcast_to(marks, (8, rows)).astype(BF16), spread, (((1,), (1,)), ((), ())),
        preferred_element_type=F32,
    )[0:1]
    copies[2].wait()
    moved = jnp.dot(spread, q_ref[...], preferred_element_type=F32)
    moved_short = moved.astype(BF16)
    own_ref[...] = moved_short[:half]
    other_ref[...] = moved_short[half:]
    packed_ref[0:half, :] = moved_short[half:, low:high]
    query_sums = row_sums(moved)
    copies[3].wait()
    packed_ref[half : half + rows, :] = k_ref[:, low:high]
    key_sums = row_sums(k_ref[...].astype(F32))
    stats_ref[...] = jnp.concatenate(
        [query_sums, key_sums, moved_marks, marks, jnp.full((4, rows), me).astype(F32)], axis=0
    )
    copies[4].wait()
    packed_ref[half + rows :, :] = v_ref[:, low:high]
    for copy in copies[5:]:
        copy.wait()


def settle_kernel(own_ref, one_ref, two_ref, three_ref, out_ref):
    out_ref[...] = (own_ref[...] + one_ref[...]) + (two_ref[...] + three_ref[...])


def pack_kernel(cut, other_ref, k_ref, v_ref, *refs):
    out_ref = refs[-1]
    low, high = cut
    half, rows = other_ref.shape[0], k_ref.shape[0]
    out_ref[0:half, :] = other_ref[:, low:high]
    out_ref[half : half + rows, :] = k_ref[:, low:high]
    out_ref[half + rows :, :] = v_ref[:, low:high]


def attend_kernel(
    cut, total_width, near_ref, far_ref, q_ref, k_ref, v_ref, qg_ref, kg_ref, remote_ref, *refs
):
    out_ref = refs[-1]
    rows = k_ref.shape[0]
    half = rows // 2
    near, far = near_ref[...], far_ref[...]
    near_factors = lax.rsqrt(near[0:2] / total_width + 1e-06)
    far_factors = lax.rsqrt(far[0:2] / total_width + 1e-06)
    q_mark = jnp.concatenate([near[2:3, :half], far[2:3, half:]], axis=1)
    k_mark = jnp.concatenate([near[3:4], far[3:4]], axis=1)
    q_factor = column(jnp.concatenate([near_factors[0:1, :half], far_factors[0:1, half:]], axis=1))
    k_factor = column(jnp.concatenate([near_factors[1:2], far_factors[1:2]], axis=1))
    lane_video = 4.0 * lax.broadcasted_iota(jnp.int32, (2 * rows, HD), 1).astype(F32)
    q_video = jnp.where(column(q_mark) == lane_video[:rows], 1.0, 0.0).astype(BF16)
    k_video = jnp.where(column(k_mark) == lane_video, 0.0, -(2.0**20)).astype(BF16)
    ones = jnp.ones((2 * rows, HD), BF16)
    scale = math.log2(math.e) / math.sqrt(HD)
    first, last = cut
    for low in range(first, last, HD):
        here = slice(low - first, low - first + HD)
        wide = slice(low, low + HD)
        queries = jnp.concatenate([q_ref[:, wide], remote_ref[0:half, here]], axis=0)
        keys = jnp.concatenate([k_ref[:, wide], remote_ref[half : half + rows, here]], axis=0)
        values = jnp.concatenate([v_ref[:, wide], remote_ref[half + rows :, here]], axis=0)
        queries = (queries.astype(F32) * q_factor * qg_ref[0:1, wide]).astype(BF16)
        keys = (keys.astype(F32) * k_factor * kg_ref[0:1, wide]).astype(BF16)
        queries = jnp.concatenate([queries, q_video], axis=1)
        keys = jnp.concatenate([keys, k_video], axis=1)
        values = jnp.concatenate([values, ones], axis=1)
        for part in range(2):
            piece = slice(part * half, (part + 1) * half)
            scores = lax.dot_general(
                queries[piece], keys, (((1,), (1,)), ((), ())), preferred_element_type=F32
            )
            largest = jnp.max(scores, axis=1, keepdims=True)
            weights = jnp.exp2((scores - largest) * scale).astype(BF16)
            mixed = jnp.dot(weights, values, preferred_element_type=F32)
            mixed, totals = mixed[:, :HD], mixed[:, HD:]
            out_ref[piece, here] = (mixed / totals).astype(BF16)


def join_kernel(count, *refs):
    low = 0
    for ref in refs[:count]:
        refs[-1][low : low + ref.shape[0], :] = ref[...]
        low += ref.shape[0]


def gate_kernel(*refs):
    refs[-1][...] = jnp.zeros(refs[-1].shape, F32)


def gate(after, weight, name):
    return pl.pallas_call(
        gate_kernel,
        in_specs=[AFTER] * len(after),
        out_specs=VMEM,
        out_shape=jax.ShapeDtypeStruct((8, 128), F32),
        compiler_params=params(4),
        cost_estimate=pl.CostEstimate(flops=weight * 900_000_000, bytes_accessed=4096, transcendentals=0),
        name=name,
    )(*after)


def join(pieces, after, name):
    return pl.pallas_call(
        functools.partial(join_kernel, len(pieces)),
        in_specs=[VMEM] * len(pieces) + [AFTER] * len(after),
        out_specs=VMEM,
        out_shape=jax.ShapeDtypeStruct((sum([piece.shape[0] for piece in pieces]), pieces[0].shape[1]), BF16),
        compiler_params=params(4),
        cost_estimate=cost(1),
        name=name,
    )(*pieces, *after)


def project_kernel(place, times, gate_ref, weight_ref, *refs):
    parts, shares = refs[:7], refs[7:13]
    total, tail_ref, gates_ref, rows_all, w_all, sems = refs[13:]
    width = total.shape[1]
    group = w_all.shape[0] // 4
    share = group // 8
    mine = place[2]
    own_start = pl.multiple_of(place[1] * width, width)
    own_copy = pltpu.make_async_copy(
        weight_ref.at[:, pl.ds(own_start, width)], w_all.at[pl.ds(0, group), :], sems.at[0]
    )
    own_copy.start()
    used = 0
    for part in parts:
        rows_all[:, used : used + part.shape[1]] = part[...]
        used += part.shape[1]
    chosen = [gate_ref[pl.ds(times[video], 1), :] for video in range(times.shape[0])]
    chosen.append(jnp.zeros((16 - len(chosen), width), F32))
    chosen = jnp.concatenate(chosen, axis=0)
    gates_ref[...] = jnp.concatenate(three_pieces(chosen), axis=0).astype(BF16)
    for core in range(2):
        near, far, other = shares[3 * core : 3 * core + 3]
        pieces = [(near, 0, 0, 0), (far, 0, 0, 4)]
        for step in (1, 2):
            pieces += [
                (near, (step + 1) * share, step, 0),
                (far, (step + 1) * share, step, 4),
                (other, (step - 1) * share, step, 1),
                (other, (step + 1) * share, step, 5),
            ]
        for ref, low, step, flip in pieces:
            count = share if step else 2 * share
            index = mine ^ (flip + 2 * core) if step else place[3] ^ (flip // 2 + core)
            start = pl.multiple_of((1 + step) * group + index * count, share)
            w_all[pl.ds(start, count), :] = ref[low : low + count, :]
    tail_ref[...] = w_all[used:, :]
    own_copy.wait()
    for low in range(0, width, 256):
        block = slice(low, low + 256)
        total[:, block] = jnp.dot(rows_all[...], w_all[0:used, block], preferred_element_type=F32)


def finish_kernel(near_ref, far_ref, total, tail_ref, gates_ref, late_ref, out_hbm, out_ref, sems):
    rows, width = out_ref.shape
    half = rows // 2
    second = near_ref[4:5, 0:1] > 0.5
    videos = lax.rem(lax.broadcasted_iota(jnp.int32, (rows, gates_ref.shape[0]), 1), 16).astype(F32)
    marks = jnp.concatenate([near_ref[2:3, :half], far_ref[2:3, half:]], axis=1)
    picked = (column(marks) == 4.0 * videos).astype(BF16)
    copies = []
    for low in range(0, width, 256):
        block = slice(low, low + 256)
        gates = jnp.dot(picked, gates_ref[:, block], preferred_element_type=F32)
        mixed = total[:, block] + jnp.dot(late_ref[...], tail_ref[:, block], preferred_element_type=F32)
        gated = mixed * gates
        out_ref[0:half, block] = jnp.where(second, gated[half:], gated[:half]).astype(BF16)
        out_ref[half:, block] = jnp.where(second, gated[:half], gated[half:]).astype(BF16)
        copies.append(pltpu.make_async_copy(out_ref.at[:, block], out_hbm.at[:, block], sems.at[len(copies)]))
        copies[-1].start()
    for copy in copies:
        copy.wait()


def fast_local(
    query_raw, key_raw, value_rows, query_gain, key_gain, segment, destination, timestep, out_weight, gate_table
):
    rows, width = query_raw.shape
    half = rows // 2
    out_width = gate_table.shape[1]
    total_width = width * lax.axis_size("head")
    ctx, head, batch = lax.axis_index("ctx"), lax.axis_index("head"), lax.axis_index("batch")
    mine = batch * 2 + ctx
    place = jnp.stack([ctx, head, mine, batch]).astype(jnp.int32)
    cuts, low = [], 0
    for count in SENDS:
        cuts.append((low * HD, (low + count) * HD))
        low += count
    assert low * HD == width
    share = width // 8
    packed_shapes = [jax.ShapeDtypeStruct((half + 2 * rows, high - low), BF16) for low, high in cuts]
    in_hbm = functools.partial(pltpu.with_memory_space_constraint, memory_space=pltpu.HBM)
    weight_hbm = in_hbm(out_weight)

    own_queries, other_queries, packed, stats, keys, values, *cut_weights = pl.pallas_call(
        functools.partial(prepare_kernel, cuts[0]),
        in_specs=[ANY] + [HBM] * 6,
        out_specs=[VMEM] * 9,
        out_shape=[
            jax.ShapeDtypeStruct((half, width), BF16),
            jax.ShapeDtypeStruct((half, width), BF16),
            packed_shapes[0],
            jax.ShapeDtypeStruct((8, rows), F32),
            jax.ShapeDtypeStruct((rows, width), BF16),
            jax.ShapeDtypeStruct((rows, width), BF16),
            jax.ShapeDtypeStruct((2 * share, out_width), BF16),
            jax.ShapeDtypeStruct((share, out_width), BF16),
            jax.ShapeDtypeStruct((share, out_width), BF16),
        ],
        scratch_shapes=[
            pltpu.VMEM((rows, width), BF16),
            pltpu.VMEM((1, rows), jnp.int32),
            pltpu.VMEM((1, rows), jnp.int32),
            pltpu.SemaphoreType.DMA((8,)),
        ],
        compiler_params=params(16),
        cost_estimate=cost(2),
        name="prepare",
    )(
        place, in_hbm(query_raw), in_hbm(key_raw), in_hbm(value_rows),
        in_hbm(destination.reshape(1, rows)), in_hbm(segment.reshape(1, rows)), weight_hbm,
    )
    from_head = [lax.ppermute(cut_weights[s - 1], "head", xor_pairs(4, s)) for s in (1, 2, 3)]
    arrived = [lax.ppermute(packed, "ctx", SWAP_CTX)]
    near = pl.pallas_call(
        settle_kernel,
        in_specs=[VMEM] * 4,
        out_specs=VMEM,
        out_shape=jax.ShapeDtypeStruct((8, rows), F32),
        compiler_params=params(4),
        cost_estimate=cost(1),
        name="settle",
    )(stats, *[lax.ppermute(stats, "head", xor_pairs(4, step)) for step in (1, 2, 3)])
    far = lax.ppermute(near, "ctx", SWAP_CTX)

    def attend(cut, piece, after):
        return pl.pallas_call(
            functools.partial(attend_kernel, cut, total_width),
            in_specs=[VMEM] * 8 + [AFTER] * len(after),
            out_specs=VMEM,
            out_shape=jax.ShapeDtypeStruct((rows, cut[1] - cut[0]), BF16),
            compiler_params=params(14),
            cost_estimate=cost(8),
            name="attend",
        )(
            near, far, own_queries, keys, values, query_gain.reshape(1, width),
            key_gain.reshape(1, width), piece, *after,
        )

    def spread(attended):
        one = lax.ppermute(attended, "head", xor_pairs(4, 1))
        two = lax.ppermute(attended, "head", xor_pairs(4, 2))
        three = lax.ppermute(two, "head", xor_pairs(4, 1))
        return [attended, one, two, three]

    first = spread(attend(cuts[0], arrived[0], [gate([far, arrived[0]], 10, "ready")]))
    clear = gate([from_head[1], first[0]], 10, "clear")
    packed = pl.pallas_call(
        functools.partial(pack_kernel, cuts[1]),
        in_specs=[VMEM] * 3 + [AFTER],
        out_specs=VMEM,
        out_shape=packed_shapes[1],
        compiler_params=params(4),
        cost_estimate=cost(1),
        name="pack",
    )(other_queries, keys, values, clear)
    arrived.append(lax.ppermute(packed, "ctx", SWAP_CTX))
    landed = gate([*from_head, packed], 10, "landed")
    two_three = join(from_head[1:], [packed], "join_two")
    share0 = join(from_head, [packed], "join_all")
    share_y = lax.ppermute(two_three, "ctx", SWAP_CTX)
    share_x = lax.ppermute(share0, "batch", SWAP_X)

    token = gate(first[1:3], 10, "token")
    attended = attend(cuts[1], arrived[1], [token])
    share_y = join([share_y], [attended, share_x], "hold")
    share_xy = lax.ppermute(share_y, "batch", SWAP_X)
    last = spread(attended)
    passed = gate([first[3], *last[1:3]], 10, "passed")
    share_yxy = join([share_y, share_xy], [passed], "join_y")
    shares = [share0, share_x, share_yxy]
    shares += [lax.ppermute(value, "batch", SWAP_CORE) for value in shares]

    parts = [first[0], last[0], first[1], last[1], first[2], last[2], first[3]]
    used = 3 * width + cuts[0][1]
    total, tail_weights, gates = pl.pallas_call(
        project_kernel,
        in_specs=[SMEM, SMEM, VMEM, HBM] + [VMEM] * (len(parts) + len(shares)),
        out_specs=[VMEM] * 3,
        out_shape=[
            jax.ShapeDtypeStruct((rows, out_width), F32),
            jax.ShapeDtypeStruct((4 * width - used, out_width), BF16),
            jax.ShapeDtypeStruct((48, out_width), BF16),
        ],
        scratch_shapes=[
            pltpu.VMEM((rows, used), BF16),
            pltpu.VMEM((4 * width, out_width), BF16),
            pltpu.SemaphoreType.DMA((1,)),
        ],
        compiler_params=params(24),
        cost_estimate=cost(0),
        name="project",
    )(place, timestep, gate_table, weight_hbm, *parts, *shares)
    return pl.pallas_call(
        finish_kernel,
        in_specs=[VMEM] * 6,
        out_specs=ANY,
        out_shape=jax.ShapeDtypeStruct((rows, out_width), BF16),
        scratch_shapes=[
            pltpu.VMEM((rows, out_width), BF16),
            pltpu.SemaphoreType.DMA((out_width // 256,)),
        ],
        compiler_params=params(14),
        cost_estimate=cost(0),
        name="finish",
    )(near, far, total, tail_weights, gates, last[3])


def for_sending(array):

    def short(part):
        return part.astype(jnp.bfloat16) if part.dtype == jnp.float32 else part

    return jax.tree.map(short, array)


def attend(running, queries, query_mark, key_rows, value_part, key_mark, head_count, score_scale):
    maxima, totals, accumulated = running
    query_count = queries.shape[0]
    query_heads = queries.reshape(query_count, head_count, HD)
    key_heads = key_rows.reshape(key_rows.shape[0], head_count, HD)
    value_heads = value_part.reshape(value_part.shape[0], head_count, HD)
    scores = (
        jnp.einsum("qhd,khd->hqk", query_heads, key_heads, preferred_element_type=jnp.float32)
        * score_scale
    )
    allowed = (query_mark[:, None] == key_mark[None, :])[None]
    scores = jnp.where(allowed, scores, -1e30)
    new_max = jnp.maximum(maxima, jnp.max(scores, axis=2))
    factor = jnp.exp(maxima - new_max)
    weights = jnp.where(allowed, jnp.exp(scores - new_max[:, :, None]), 0.0)
    totals = totals * factor + jnp.sum(weights, axis=2)
    update = jnp.einsum(
        "hqk,khd->qhd",
        weights.astype(jnp.bfloat16),
        value_heads,
        preferred_element_type=jnp.float32,
    )
    accumulated = accumulated * jnp.transpose(factor)[:, :, None] + update
    return (new_max, totals, accumulated)


def attend_blocks(
    running, queries, query_mark, key_rows, value_part, key_mark, head_count, score_scale
):
    block_rows = queries.shape[0]
    block_count = key_rows.shape[0] // block_rows
    stacked = (
        key_rows.reshape(block_count, block_rows, key_rows.shape[1]),
        value_part.reshape(block_count, block_rows, value_part.shape[1]),
        key_mark.reshape(block_count, block_rows),
    )

    def advance(state, shard_piece):
        return (
            attend(
                state,
                queries,
                query_mark,
                shard_piece[0],
                shard_piece[1],
                shard_piece[2],
                head_count,
                score_scale,
            ),
            None,
        )

    running, unused = lax.scan(advance, running, stacked)
    return running


def general_local(
    query_raw,
    key_raw,
    value_rows,
    query_gain,
    key_gain,
    segment,
    destination,
    timestep,
    out_weight,
    gate_table,
):
    row_count = query_raw.shape[0]
    row_width = query_raw.shape[1]
    head_count = row_width // HD
    ctx_size = lax.axis_size("ctx")
    total_width = row_width * lax.axis_size("head")
    score_scale = 1.0 / math.sqrt(HD)
    query_float = query_raw.astype(jnp.float32)
    key_float = key_raw.astype(jnp.float32)
    query_sum, key_sum = lax.psum(
        (jnp.sum(query_float * query_float, axis=1), jnp.sum(key_float * key_float, axis=1)), "head"
    )
    queries = (
        query_float * lax.rsqrt(query_sum / total_width + 1e-06)[:, None] * query_gain
    ).astype(jnp.bfloat16)
    normed_keys = (key_float * lax.rsqrt(key_sum / total_width + 1e-06)[:, None] * key_gain).astype(
        jnp.bfloat16
    )
    slot_count = row_count // ctx_size
    target = destination // row_count * slot_count + destination % slot_count

    def placed(array):
        return jnp.zeros_like(array).at[target].set(array)

    initial = (
        jnp.full((head_count, row_count), -1e30, jnp.float32),
        jnp.zeros((head_count, row_count), jnp.float32),
        jnp.zeros((row_count, head_count, HD), jnp.float32),
    )
    own_queries, own_keys, own_values, own_segment = (
        lax.all_to_all(placed(queries), "ctx", split_axis=0, concat_axis=0, tiled=True),
        lax.all_to_all(placed(normed_keys), "ctx", split_axis=0, concat_axis=0, tiled=True),
        lax.all_to_all(placed(value_rows), "ctx", split_axis=0, concat_axis=0, tiled=True),
        lax.all_to_all(placed(segment), "ctx", split_axis=0, concat_axis=0, tiled=True),
    )
    running = attend_blocks(
        initial,
        own_queries,
        own_segment,
        lax.all_gather(own_keys, "ctx", axis=0, tiled=True),
        lax.all_gather(own_values, "ctx", axis=0, tiled=True),
        lax.all_gather(for_sending(own_segment), "ctx", axis=0, tiled=True),
        head_count,
        score_scale,
    )
    attended = (
        (running[2] / jnp.transpose(running[1])[:, :, None])
        .reshape(row_count, row_width)
        .astype(jnp.bfloat16)
    )
    head_terms = jnp.dot(attended, out_weight, preferred_element_type=jnp.float32)
    mixed_rows = lax.psum_scatter(
        head_terms.astype(jnp.bfloat16), "head", scatter_dimension=1, tiled=True
    ).astype(jnp.float32)
    video_gates = jnp.dot(
        jax.nn.one_hot(timestep, gate_table.shape[0], dtype=jnp.float32),
        gate_table,
        precision=lax.Precision.HIGHEST,
    )
    token_gates = jnp.dot(
        jax.nn.one_hot(own_segment, timestep.shape[0], dtype=jnp.float32),
        video_gates,
        precision=lax.Precision.HIGHEST,
    )
    return (mixed_rows * token_gates).astype(jnp.bfloat16)


def solution(mesh):
    placed = (
        P(("batch", "ctx"), "head"),
        P(("batch", "ctx"), "head"),
        P(("batch", "ctx"), "head"),
        P("head"),
        P("head"),
        P(("batch", "ctx")),
        P(("batch", "ctx")),
        P("batch"),
        P("head", None),
        P(None, "head"),
    )
    sizes = dict(mesh.shape)
    fast = sizes["batch"] == 4 and sizes["ctx"] == 2 and sizes["head"] == 4
    local = fast_local if fast else general_local
    return jax.shard_map(
        local, mesh=mesh, in_specs=placed, out_specs=P(("batch", "ctx"), "head"), check_vma=False
    )
```

```python
import functools
import math

import jax
import jax.numpy as jnp
from jax import lax
from jax.experimental import pallas as pl
from jax.experimental.pallas import tpu as pltpu
from jax.sharding import PartitionSpec as P

HD = 128
F32 = jnp.float32
BF16 = jnp.bfloat16
VMEM = pl.BlockSpec(memory_space=pltpu.VMEM)
SMEM = pl.BlockSpec(memory_space=pltpu.SMEM)
ANY = pl.BlockSpec(memory_space=pl.ANY)
HBM = pl.BlockSpec(memory_space=pltpu.HBM)
AFTER = VMEM
SENDS = (3, 2)

SWAP_CTX = ((0, 1), (1, 0))
SWAP_CORE = ((0, 1), (1, 0), (2, 3), (3, 2))
SWAP_X = ((0, 2), (2, 0), (1, 3), (3, 1))


def xor_pairs(size, step):
    return tuple((i, i ^ step) for i in range(size))


def params(mebibytes):
    return pltpu.CompilerParams(vmem_limit_bytes=mebibytes * 1024 * 1024)


def cost(microseconds):
    return pl.CostEstimate(flops=0, bytes_accessed=int(microseconds * 3_600_000), transcendentals=0)


def load(pairs, sems):
    copies = [pltpu.make_async_copy(source, target, sems.at[i]) for i, (source, target) in enumerate(pairs)]
    for copy in copies:
        copy.start()
    return copies


def row_sums(values):
    squares = values * values
    folded = squares[:, 0:HD]
    for low in range(HD, values.shape[1], HD):
        folded = folded + squares[:, low : low + HD]
    return jnp.sum(jnp.transpose(folded), axis=0, keepdims=True)


def three_pieces(value):
    pieces = []
    for _ in range(3):
        short = value.astype(BF16).astype(F32)
        pieces.append(short)
        value = value - short
    return pieces


def column(row):
    return jnp.transpose(jnp.broadcast_to(row, (8, row.shape[1])))[:, 0:1]


def prepare_kernel(
    cut, after_ref, q_hbm, k_hbm, v_hbm, dest_hbm, seg_hbm, weight_ref,
    own_ref, other_ref, packed_ref, stats_ref, k_ref, v_ref, one_ref, two_ref, three_ref,
    q_ref, dest_ref, seg_ref, sems,
):
    me, head, batch = lax.axis_index("ctx"), lax.axis_index("head"), lax.axis_index("batch")
    mine = batch * 2 + me
    pairs = [(dest_hbm, dest_ref), (seg_hbm, seg_ref), (q_hbm, q_ref), (k_hbm, k_ref), (v_hbm, v_ref)]
    for step, (ref, index) in enumerate(((one_ref, batch), (two_ref, mine), (three_ref, mine))):
        count, columns = ref.shape
        first = pl.multiple_of(index * count, count)
        start = pl.multiple_of((head ^ (step + 1)) * columns, columns)
        pairs.append((weight_ref.at[pl.ds(first, count), pl.ds(start, columns)], ref))
    copies = load(pairs, sems)
    rows = q_ref.shape[0]
    half = rows // 2
    low, high = cut
    copies[0].wait()
    copies[1].wait()
    dest = dest_ref[...]
    block = (dest >= rows).astype(jnp.int32)
    slot = dest - block * rows - me * half + jnp.where(block == me, 0, half)
    spread = (lax.broadcasted_iota(jnp.int32, (rows, rows), 0) == slot).astype(BF16)
    marks = seg_ref[...].astype(F32)
    moved_marks = lax.dot_general(
        jnp.broadcast_to(marks, (8, rows)).astype(BF16), spread, (((1,), (1,)), ((), ())),
        preferred_element_type=F32,
    )[0:1]
    copies[2].wait()
    moved = jnp.dot(spread, q_ref[...], preferred_element_type=F32)
    moved_short = moved.astype(BF16)
    own_ref[...] = moved_short[:half]
    other_ref[...] = moved_short[half:]
    packed_ref[0:half, :] = moved_short[half:, low:high]
    query_sums = row_sums(moved)
    copies[3].wait()
    packed_ref[half : half + rows, :] = k_ref[:, low:high]
    key_sums = row_sums(k_ref[...].astype(F32))
    stats_ref[...] = jnp.concatenate(
        [query_sums, key_sums, moved_marks, marks, jnp.full((4, rows), me).astype(F32)], axis=0
    )
    copies[4].wait()
    packed_ref[half + rows :, :] = v_ref[:, low:high]
    for copy in copies[5:]:
        copy.wait()


def settle_kernel(own_ref, one_ref, two_ref, three_ref, out_ref):
    out_ref[...] = (own_ref[...] + one_ref[...]) + (two_ref[...] + three_ref[...])


def pack_kernel(cut, other_ref, k_ref, v_ref, *refs):
    out_ref = refs[-1]
    low, high = cut
    half, rows = other_ref.shape[0], k_ref.shape[0]
    out_ref[0:half, :] = other_ref[:, low:high]
    out_ref[half : half + rows, :] = k_ref[:, low:high]
    out_ref[half + rows :, :] = v_ref[:, low:high]


def attend_kernel(
    cut, total_width, near_ref, far_ref, q_ref, k_ref, v_ref, qg_ref, kg_ref, remote_ref, *refs
):
    out_ref = refs[-1]
    rows = k_ref.shape[0]
    half = rows // 2
    near, far = near_ref[...], far_ref[...]
    near_factors = lax.rsqrt(near[0:2] / total_width + 1e-06)
    far_factors = lax.rsqrt(far[0:2] / total_width + 1e-06)
    q_mark = jnp.concatenate([near[2:3, :half], far[2:3, half:]], axis=1)
    k_mark = jnp.concatenate([near[3:4], far[3:4]], axis=1)
    q_factor = column(jnp.concatenate([near_factors[0:1, :half], far_factors[0:1, half:]], axis=1))
    k_factor = column(jnp.concatenate([near_factors[1:2], far_factors[1:2]], axis=1))
    lane_video = 4.0 * lax.broadcasted_iota(jnp.int32, (2 * rows, HD), 1).astype(F32)
    q_video = jnp.where(column(q_mark) == lane_video[:rows], 1.0, 0.0).astype(BF16)
    k_video = jnp.where(column(k_mark) == lane_video, 0.0, -(2.0**20)).astype(BF16)
    ones = jnp.ones((2 * rows, HD), BF16)
    scale = math.log2(math.e) / math.sqrt(HD)
    first, last = cut
    for low in range(first, last, HD):
        here = slice(low - first, low - first + HD)
        wide = slice(low, low + HD)
        queries = jnp.concatenate([q_ref[:, wide], remote_ref[0:half, here]], axis=0)
        keys = jnp.concatenate([k_ref[:, wide], remote_ref[half : half + rows, here]], axis=0)
        values = jnp.concatenate([v_ref[:, wide], remote_ref[half + rows :, here]], axis=0)
        queries = (queries.astype(F32) * q_factor * qg_ref[0:1, wide]).astype(BF16)
        keys = (keys.astype(F32) * k_factor * kg_ref[0:1, wide]).astype(BF16)
        queries = jnp.concatenate([queries, q_video], axis=1)
        keys = jnp.concatenate([keys, k_video], axis=1)
        values = jnp.concatenate([values, ones], axis=1)
        for part in range(2):
            piece = slice(part * half, (part + 1) * half)
            scores = lax.dot_general(
                queries[piece], keys, (((1,), (1,)), ((), ())), preferred_element_type=F32
            )
            largest = jnp.max(scores, axis=1, keepdims=True)
            weights = jnp.exp2((scores - largest) * scale).astype(BF16)
            mixed = jnp.dot(weights, values, preferred_element_type=F32)
            mixed, totals = mixed[:, :HD], mixed[:, HD:]
            out_ref[piece, here] = (mixed / totals).astype(BF16)


def join_kernel(count, *refs):
    low = 0
    for ref in refs[:count]:
        refs[-1][low : low + ref.shape[0], :] = ref[...]
        low += ref.shape[0]


def gate_kernel(*refs):
    refs[-1][...] = jnp.zeros(refs[-1].shape, F32)


def gate(after, weight, name):
    return pl.pallas_call(
        gate_kernel,
        in_specs=[AFTER] * len(after),
        out_specs=VMEM,
        out_shape=jax.ShapeDtypeStruct((8, 128), F32),
        compiler_params=params(4),
        cost_estimate=pl.CostEstimate(flops=weight * 900_000_000, bytes_accessed=4096, transcendentals=0),
        name=name,
    )(*after)


def join(pieces, after, name):
    return pl.pallas_call(
        functools.partial(join_kernel, len(pieces)),
        in_specs=[VMEM] * len(pieces) + [AFTER] * len(after),
        out_specs=VMEM,
        out_shape=jax.ShapeDtypeStruct((sum([piece.shape[0] for piece in pieces]), pieces[0].shape[1]), BF16),
        compiler_params=params(4),
        cost_estimate=cost(1),
        name=name,
    )(*pieces, *after)


def own_kernel(after_ref, later_ref, weight_ref, first_ref, last_ref, out_ref, own_w, sems):
    width = out_ref.shape[1]
    start = pl.multiple_of(lax.axis_index("head") * width, width)
    copy = pltpu.make_async_copy(weight_ref.at[:, pl.ds(start, width)], own_w, sems.at[0])
    copy.start()
    rows = jnp.concatenate([first_ref[...], last_ref[...]], axis=1)
    copy.wait()
    for low in range(0, width, 256):
        block = slice(low, low + 256)
        out_ref[:, block] = jnp.dot(rows, own_w[:, block], preferred_element_type=F32)


def project_kernel(after_ref, times, gate_ref, own_total, *refs):
    parts, shares = refs[:5], refs[5:11]
    total, tail_ref, gates_ref, rows_all, w_all = refs[11:]
    width = total.shape[1]
    group = w_all.shape[0] // 3
    share = group // 8
    batch = lax.axis_index("batch")
    mine = batch * 2 + lax.axis_index("ctx")
    used = 0
    for part in parts:
        rows_all[:, used : used + part.shape[1]] = part[...]
        used += part.shape[1]
    chosen = [gate_ref[pl.ds(times[video], 1), :] for video in range(times.shape[0])]
    chosen.append(jnp.zeros((16 - len(chosen), width), F32))
    chosen = jnp.concatenate(chosen, axis=0)
    gates_ref[...] = jnp.concatenate(three_pieces(chosen), axis=0).astype(BF16)
    for core in range(2):
        near, far, other = shares[3 * core : 3 * core + 3]
        pieces = [(near, 0, 0, 0), (far, 0, 0, 4)]
        for step in (1, 2):
            pieces += [
                (near, (step + 1) * share, step, 0),
                (far, (step + 1) * share, step, 4),
                (other, (step - 1) * share, step, 1),
                (other, (step + 1) * share, step, 5),
            ]
        for ref, low, step, flip in pieces:
            count = share if step else 2 * share
            index = mine ^ (flip + 2 * core) if step else batch ^ (flip // 2 + core)
            start = pl.multiple_of(step * group + index * count, share)
            w_all[pl.ds(start, count), :] = ref[low : low + count, :]
    tail_ref[...] = w_all[used:, :]
    for low in range(0, width, 256):
        block = slice(low, low + 256)
        total[:, block] = own_total[:, block] + jnp.dot(rows_all[...], w_all[0:used, block], preferred_element_type=F32)


def finish_kernel(near_ref, far_ref, total, tail_ref, gates_ref, late_ref, out_hbm, out_ref, sems):
    rows, width = out_ref.shape
    half = rows // 2
    second = near_ref[4:5, 0:1] > 0.5
    videos = lax.rem(lax.broadcasted_iota(jnp.int32, (rows, gates_ref.shape[0]), 1), 16).astype(F32)
    marks = jnp.concatenate([near_ref[2:3, :half], far_ref[2:3, half:]], axis=1)
    picked = (column(marks) == 4.0 * videos).astype(BF16)
    copies = []
    for low in range(0, width, 256):
        block = slice(low, low + 256)
        gates = jnp.dot(picked, gates_ref[:, block], preferred_element_type=F32)
        mixed = total[:, block] + jnp.dot(late_ref[...], tail_ref[:, block], preferred_element_type=F32)
        gated = mixed * gates
        out_ref[0:half, block] = jnp.where(second, gated[half:], gated[:half]).astype(BF16)
        out_ref[half:, block] = jnp.where(second, gated[:half], gated[half:]).astype(BF16)
        copies.append(pltpu.make_async_copy(out_ref.at[:, block], out_hbm.at[:, block], sems.at[len(copies)]))
        copies[-1].start()
    for copy in copies:
        copy.wait()


def fast_local(
    query_raw, key_raw, value_rows, query_gain, key_gain, segment, destination, timestep, out_weight, gate_table
):
    rows, width = query_raw.shape
    half = rows // 2
    out_width = gate_table.shape[1]
    total_width = width * lax.axis_size("head")
    ctx, head, batch = lax.axis_index("ctx"), lax.axis_index("head"), lax.axis_index("batch")
    mine = batch * 2 + ctx
    place = jnp.stack([ctx, head, mine, batch]).astype(jnp.int32)
    cuts, low = [], 0
    for count in SENDS:
        cuts.append((low * HD, (low + count) * HD))
        low += count
    assert low * HD == width
    share = width // 8
    packed_shapes = [jax.ShapeDtypeStruct((half + 2 * rows, high - low), BF16) for low, high in cuts]
    in_hbm = functools.partial(pltpu.with_memory_space_constraint, memory_space=pltpu.HBM)
    weight_hbm = in_hbm(out_weight)

    own_queries, other_queries, packed, stats, keys, values, *cut_weights = pl.pallas_call(
        functools.partial(prepare_kernel, cuts[0]),
        in_specs=[ANY] + [HBM] * 6,
        out_specs=[VMEM] * 9,
        out_shape=[
            jax.ShapeDtypeStruct((half, width), BF16),
            jax.ShapeDtypeStruct((half, width), BF16),
            packed_shapes[0],
            jax.ShapeDtypeStruct((8, rows), F32),
            jax.ShapeDtypeStruct((rows, width), BF16),
            jax.ShapeDtypeStruct((rows, width), BF16),
            jax.ShapeDtypeStruct((2 * share, out_width), BF16),
            jax.ShapeDtypeStruct((share, out_width), BF16),
            jax.ShapeDtypeStruct((share, out_width), BF16),
        ],
        scratch_shapes=[
            pltpu.VMEM((rows, width), BF16),
            pltpu.VMEM((1, rows), jnp.int32),
            pltpu.VMEM((1, rows), jnp.int32),
            pltpu.SemaphoreType.DMA((8,)),
        ],
        compiler_params=params(16),
        cost_estimate=cost(2),
        name="prepare",
    )(
        place, in_hbm(query_raw), in_hbm(key_raw), in_hbm(value_rows),
        in_hbm(destination.reshape(1, rows)), in_hbm(segment.reshape(1, rows)), weight_hbm,
    )
    from_head = [lax.ppermute(cut_weights[s - 1], "head", xor_pairs(4, s)) for s in (1, 2, 3)]
    arrived = [lax.ppermute(packed, "ctx", SWAP_CTX)]
    near = pl.pallas_call(
        settle_kernel,
        in_specs=[VMEM] * 4,
        out_specs=VMEM,
        out_shape=jax.ShapeDtypeStruct((8, rows), F32),
        compiler_params=params(4),
        cost_estimate=cost(1),
        name="settle",
    )(stats, *[lax.ppermute(stats, "head", xor_pairs(4, step)) for step in (1, 2, 3)])
    far = lax.ppermute(near, "ctx", SWAP_CTX)

    def attend(cut, piece, after):
        return pl.pallas_call(
            functools.partial(attend_kernel, cut, total_width),
            in_specs=[VMEM] * 8 + [AFTER] * len(after),
            out_specs=VMEM,
            out_shape=jax.ShapeDtypeStruct((rows, cut[1] - cut[0]), BF16),
            compiler_params=params(14),
            cost_estimate=cost(8),
            name="attend",
        )(
            near, far, own_queries, keys, values, query_gain.reshape(1, width),
            key_gain.reshape(1, width), piece, *after,
        )

    def spread(attended):
        one = lax.ppermute(attended, "head", xor_pairs(4, 1))
        two = lax.ppermute(attended, "head", xor_pairs(4, 2))
        three = lax.ppermute(two, "head", xor_pairs(4, 1))
        return [attended, one, two, three]

    first = spread(attend(cuts[0], arrived[0], [gate([far, arrived[0]], 10, "ready")]))
    clear = gate([from_head[1], first[0]], 10, "clear")
    packed = pl.pallas_call(
        functools.partial(pack_kernel, cuts[1]),
        in_specs=[VMEM] * 3 + [AFTER],
        out_specs=VMEM,
        out_shape=packed_shapes[1],
        compiler_params=params(4),
        cost_estimate=cost(1),
        name="pack",
    )(other_queries, keys, values, clear)
    arrived.append(lax.ppermute(packed, "ctx", SWAP_CTX))
    landed = gate([*from_head, packed], 10, "landed")
    two_three = join(from_head[1:], [packed], "join_two")
    share0 = join(from_head, [packed], "join_all")
    share_y = lax.ppermute(two_three, "ctx", SWAP_CTX)
    share_x = lax.ppermute(share0, "batch", SWAP_X)

    token = gate(first[1:3], 10, "token")
    attended = attend(cuts[1], arrived[1], [token])
    share_y = join([share_y], [attended, share_x], "hold")
    share_xy = lax.ppermute(share_y, "batch", SWAP_X)
    last = spread(attended)
    own_total = pl.pallas_call(
        own_kernel,
        in_specs=[AFTER, AFTER, HBM, VMEM, VMEM],
        out_specs=VMEM,
        out_shape=jax.ShapeDtypeStruct((rows, out_width), F32),
        scratch_shapes=[pltpu.VMEM((width, out_width), BF16), pltpu.SemaphoreType.DMA((1,))],
        compiler_params=params(14),
        cost_estimate=cost(0),
        name="own",
    )(first[3], share_y, weight_hbm, first[0], last[0])
    passed = gate([first[3], *last[1:3], own_total], 10, "passed")
    share_yxy = join([share_y, share_xy], [passed], "join_y")
    shares = [share0, share_x, share_yxy]
    shares += [lax.ppermute(value, "batch", SWAP_CORE) for value in shares]

    parts = [first[1], last[1], first[2], last[2], first[3]]
    used = 2 * width + cuts[0][1]
    total, tail_weights, gates = pl.pallas_call(
        project_kernel,
        in_specs=[ANY, SMEM, VMEM, VMEM] + [VMEM] * (len(parts) + len(shares)),
        out_specs=[VMEM] * 3,
        out_shape=[
            jax.ShapeDtypeStruct((rows, out_width), F32),
            jax.ShapeDtypeStruct((3 * width - used, out_width), BF16),
            jax.ShapeDtypeStruct((48, out_width), BF16),
        ],
        scratch_shapes=[
            pltpu.VMEM((rows, used), BF16),
            pltpu.VMEM((3 * width, out_width), BF16),
        ],
        compiler_params=params(24),
        cost_estimate=cost(0),
        name="project",
    )(place, timestep, gate_table, own_total, *parts, *shares)
    return pl.pallas_call(
        finish_kernel,
        in_specs=[VMEM] * 6,
        out_specs=ANY,
        out_shape=jax.ShapeDtypeStruct((rows, out_width), BF16),
        scratch_shapes=[
            pltpu.VMEM((rows, out_width), BF16),
            pltpu.SemaphoreType.DMA((out_width // 256,)),
        ],
        compiler_params=params(14),
        cost_estimate=cost(0),
        name="finish",
    )(near, far, total, tail_weights, gates, last[3])


def for_sending(array):

    def short(part):
        return part.astype(jnp.bfloat16) if part.dtype == jnp.float32 else part

    return jax.tree.map(short, array)


def attend(running, queries, query_mark, key_rows, value_part, key_mark, head_count, score_scale):
    maxima, totals, accumulated = running
    query_count = queries.shape[0]
    query_heads = queries.reshape(query_count, head_count, HD)
    key_heads = key_rows.reshape(key_rows.shape[0], head_count, HD)
    value_heads = value_part.reshape(value_part.shape[0], head_count, HD)
    scores = (
        jnp.einsum("qhd,khd->hqk", query_heads, key_heads, preferred_element_type=jnp.float32)
        * score_scale
    )
    allowed = (query_mark[:, None] == key_mark[None, :])[None]
    scores = jnp.where(allowed, scores, -1e30)
    new_max = jnp.maximum(maxima, jnp.max(scores, axis=2))
    factor = jnp.exp(maxima - new_max)
    weights = jnp.where(allowed, jnp.exp(scores - new_max[:, :, None]), 0.0)
    totals = totals * factor + jnp.sum(weights, axis=2)
    update = jnp.einsum(
        "hqk,khd->qhd",
        weights.astype(jnp.bfloat16),
        value_heads,
        preferred_element_type=jnp.float32,
    )
    accumulated = accumulated * jnp.transpose(factor)[:, :, None] + update
    return (new_max, totals, accumulated)


def attend_blocks(
    running, queries, query_mark, key_rows, value_part, key_mark, head_count, score_scale
):
    block_rows = queries.shape[0]
    block_count = key_rows.shape[0] // block_rows
    stacked = (
        key_rows.reshape(block_count, block_rows, key_rows.shape[1]),
        value_part.reshape(block_count, block_rows, value_part.shape[1]),
        key_mark.reshape(block_count, block_rows),
    )

    def advance(state, shard_piece):
        return (
            attend(
                state,
                queries,
                query_mark,
                shard_piece[0],
                shard_piece[1],
                shard_piece[2],
                head_count,
                score_scale,
            ),
            None,
        )

    running, unused = lax.scan(advance, running, stacked)
    return running


def general_local(
    query_raw,
    key_raw,
    value_rows,
    query_gain,
    key_gain,
    segment,
    destination,
    timestep,
    out_weight,
    gate_table,
):
    row_count = query_raw.shape[0]
    row_width = query_raw.shape[1]
    head_count = row_width // HD
    ctx_size = lax.axis_size("ctx")
    total_width = row_width * lax.axis_size("head")
    score_scale = 1.0 / math.sqrt(HD)
    query_float = query_raw.astype(jnp.float32)
    key_float = key_raw.astype(jnp.float32)
    query_sum, key_sum = lax.psum(
        (jnp.sum(query_float * query_float, axis=1), jnp.sum(key_float * key_float, axis=1)), "head"
    )
    queries = (
        query_float * lax.rsqrt(query_sum / total_width + 1e-06)[:, None] * query_gain
    ).astype(jnp.bfloat16)
    normed_keys = (key_float * lax.rsqrt(key_sum / total_width + 1e-06)[:, None] * key_gain).astype(
        jnp.bfloat16
    )
    slot_count = row_count // ctx_size
    target = destination // row_count * slot_count + destination % slot_count

    def placed(array):
        return jnp.zeros_like(array).at[target].set(array)

    initial = (
        jnp.full((head_count, row_count), -1e30, jnp.float32),
        jnp.zeros((head_count, row_count), jnp.float32),
        jnp.zeros((row_count, head_count, HD), jnp.float32),
    )
    own_queries, own_keys, own_values, own_segment = (
        lax.all_to_all(placed(queries), "ctx", split_axis=0, concat_axis=0, tiled=True),
        lax.all_to_all(placed(normed_keys), "ctx", split_axis=0, concat_axis=0, tiled=True),
        lax.all_to_all(placed(value_rows), "ctx", split_axis=0, concat_axis=0, tiled=True),
        lax.all_to_all(placed(segment), "ctx", split_axis=0, concat_axis=0, tiled=True),
    )
    running = attend_blocks(
        initial,
        own_queries,
        own_segment,
        lax.all_gather(own_keys, "ctx", axis=0, tiled=True),
        lax.all_gather(own_values, "ctx", axis=0, tiled=True),
        lax.all_gather(for_sending(own_segment), "ctx", axis=0, tiled=True),
        head_count,
        score_scale,
    )
    attended = (
        (running[2] / jnp.transpose(running[1])[:, :, None])
        .reshape(row_count, row_width)
        .astype(jnp.bfloat16)
    )
    head_terms = jnp.dot(attended, out_weight, preferred_element_type=jnp.float32)
    mixed_rows = lax.psum_scatter(
        head_terms.astype(jnp.bfloat16), "head", scatter_dimension=1, tiled=True
    ).astype(jnp.float32)
    video_gates = jnp.dot(
        jax.nn.one_hot(timestep, gate_table.shape[0], dtype=jnp.float32),
        gate_table,
        precision=lax.Precision.HIGHEST,
    )
    token_gates = jnp.dot(
        jax.nn.one_hot(own_segment, timestep.shape[0], dtype=jnp.float32),
        video_gates,
        precision=lax.Precision.HIGHEST,
    )
    return (mixed_rows * token_gates).astype(jnp.bfloat16)


def solution(mesh):
    placed = (
        P(("batch", "ctx"), "head"),
        P(("batch", "ctx"), "head"),
        P(("batch", "ctx"), "head"),
        P("head"),
        P("head"),
        P(("batch", "ctx")),
        P(("batch", "ctx")),
        P("batch"),
        P("head", None),
        P(None, "head"),
    )
    sizes = dict(mesh.shape)
    fast = sizes["batch"] == 4 and sizes["ctx"] == 2 and sizes["head"] == 4
    local = fast_local if fast else general_local
    return jax.shard_map(
        local, mesh=mesh, in_specs=placed, out_specs=P(("batch", "ctx"), "head"), check_vma=False
    )
```
